32 devices in a mesh: rows: 8 (over z, x), cols: 4 (over y, core).
Axes of the slice: x: 2, y: 2, z: 4, core: 2. Of those that a mesh axis runs over, the one named last changes fastest.
Arguments:
- panel_cols: bfloat16 [32, 16, 256, 128], P('rows', 'cols'), may hold values from -2 to 2
- pivot_inv: bfloat16 [16, 256, 256], P('cols'), may hold values from -0.375 to 0.375
- pivot_rows: bfloat16 [16, 24, 256, 128], P('rows', 'cols'), may hold values from -2 to 2
- target_factors: bfloat16 [32, 24, 256, 128], P('rows', 'cols'), may hold values from -5 to 5
- near_blocks: bfloat16 [32, 4, 256, 256], P('rows', 'cols'), may hold values from -6 to 6
- near_cols: int32 [32, 4], P('rows', 'cols'), may hold values from 0 to 5, as said below
- sketch: bfloat16 [24, 256, 64], P('cols'), may hold values from -6 to 6
Outputs:
- near_out: bfloat16 [32, 4, 256, 256], P('rows', 'cols')
- far_out: bfloat16 [32, 24, 256, 128], P('rows', 'cols')
The draws below stay inside these ranges and needn't reach their ends.
Inputs may be any that keep to these rules, and one draw needn't show every extreme that they name: `near_cols`: for every block row, the 1 entries of each group of slots s with equal s // 1 are distinct.
All inputs are finite; a program needn't handle non-finite values.
Results may differ from the reference program's by a relative error of at most 0.009.
Values may be sent and summed in bfloat16 or wider, within the bound.
No kernel may reach another device: no remote copies, remote signals or barrier semaphores. Data moves between devices by JAX's collectives and lax.ppermute only.
A program may use at most 128 MiB of HBM per device.

```python
import math
import jax
import jax.numpy as jnp
from jax import lax

B = 256
R = 64
CB_DEV = 6
NNEAR_DEV = 1
KP = 16
NBR = 32
NBC = 24
NNEAR = 4
N_COLS = 4


def draw_near_cols(key, part):
    scores = jax.random.randint(key, (NBR, N_COLS, CB_DEV), 0, 65536)
    scores = scores * CB_DEV + jnp.arange(CB_DEV, dtype=jnp.int32)[None, None, :]
    order = jnp.argsort(scores, axis=-1)
    chosen = order[:, :, :NNEAR_DEV]
    return chosen.reshape(NBR, N_COLS * NNEAR_DEV).astype(jnp.int32)


def shard_levels(rng, extent, cuts, smallest, top_value):
    gain = 1.0
    for position, shards_of in cuts:
        steps = jax.random.uniform(jax.random.fold_in(jax.random.fold_in(rng, 6), position), (shards_of,), jnp.float32, smallest / len(cuts), top_value / len(cuts))
        gain = gain * jnp.repeat(jnp.exp(steps), extent[position] // shards_of).reshape((-1,) + (1,) * (len(extent) - 1 - position))
    return gain


def scatter_about(stream_key, dims, spread, reach, pieces=(), held_as=jnp.bfloat16):
    result = jax.random.normal(stream_key, dims, jnp.float32) * spread
    if len(pieces) > 0:
        result = shard_levels(stream_key, dims, pieces, -0.22, 0.18) * result
    return jnp.clip(result, min=-reach, max=reach).astype(held_as)


def setup_inputs(seed: int = 0) -> dict:
    seeds = jax.random.split(jax.random.key(seed), 8)
    return {
        "panel_cols": scatter_about(seeds[0], (NBR, KP, B, 2 * R), ((B * R * R * KP) ** -0.125), 2.0, ((0, 8), (1, 4))),
        "pivot_inv": scatter_about(seeds[1], (KP, B, B), B ** -0.5, 0.375, ((0, 4),)),
        "pivot_rows": scatter_about(seeds[2], (KP, NBC, B, 2 * R), ((B * R * R * KP) ** -0.125), 2.0, ((0, 8), (1, 4))),
        "target_factors": scatter_about(seeds[3], (NBR, NBC, B, 2 * R), 0.35, 5.0, ((0, 8), (1, 4))),
        "near_blocks": scatter_about(seeds[4], (NBR, NNEAR, B, B), 1.0, 6.0, ((0, 8), (1, 4))),
        "near_cols": draw_near_cols(jax.random.fold_in(seeds[7], 71), 0),
        "sketch": scatter_about(seeds[6], (NBC, B, R), 1.0, 6.0, ((0, 4),)),
    }


def product_of(form, left, right):
    return jnp.einsum(form, left.astype(jnp.float32), right.astype(jnp.float32), precision=lax.Precision.HIGHEST)

def row_update(left_row, rows_all, target_row, near_row, near_index, sketch):
    half = left_row.shape[-1] // 2
    root_size = math.sqrt(left_row.shape[1])
    left_x = left_row[..., :half]
    left_y = left_row[..., half:]
    pivot_p = rows_all[..., :half]
    pivot_q = rows_all[..., half:]
    mid_cores = product_of('kbr,kjbs->kjrs', left_y, pivot_p).astype(jnp.bfloat16)
    left_terms = product_of('kbr,kjrs->jkbs', left_x, mid_cores).astype(jnp.bfloat16)
    left_near = jnp.take(left_terms, near_index, axis=0)
    q_near = jnp.take(pivot_q, near_index, axis=1)
    update = product_of('nkbs,kncs->nbc', left_near, q_near)
    near_new = (near_row.astype(jnp.float32) - update).astype(jnp.bfloat16)
    column_ids = jnp.arange(target_row.shape[0], dtype=jnp.int32)
    is_near = jnp.any(near_index[:, None] == column_ids[None, :], axis=0)
    target_u = target_row[..., :half]
    target_v = target_row[..., half:]
    sketch_core = product_of('jbs,jbt->jst', target_v, sketch).astype(jnp.bfloat16)
    pivot_sketch = product_of('kjbs,jbt->jkst', pivot_q, sketch).astype(jnp.bfloat16)
    sampled = product_of('jbs,jst->jbt', target_u, sketch_core) - product_of('jkbs,jkst->jbt', left_terms, pivot_sketch)
    gram_matrix = jnp.einsum('jbs,jbt->jst', sampled, sampled, precision=lax.Precision.HIGHEST)
    factor_chol = jnp.linalg.cholesky(gram_matrix)
    orthonormal = lax.linalg.triangular_solve(factor_chol, sampled, left_side=False, lower=True, transpose_a=True)
    basis = (root_size * orthonormal).astype(jnp.bfloat16)
    basis_core = product_of('jbs,jbt->jst', target_u, basis).astype(jnp.bfloat16)
    left_core = product_of('jkbs,jbt->jkst', left_terms, basis).astype(jnp.bfloat16)
    weights_out = (product_of('jbs,jst->jbt', target_v, basis_core) - product_of('kjbs,jkst->jbt', pivot_q, left_core)) / root_size
    keep_far = jnp.where(is_near, 0.0, 1.0).astype(jnp.bfloat16)[:, None, None]
    far_new = jnp.concatenate([basis, weights_out.astype(jnp.bfloat16)], axis=-1) * keep_far
    return (near_new, far_new)

def reference(panel_cols, pivot_inv, pivot_rows, target_factors, near_blocks, near_cols, sketch):
    half = panel_cols.shape[-1] // 2
    col_left = panel_cols[..., :half]
    col_right = panel_cols[..., half:]
    pivot_right = product_of('kab,ikar->ikbr', pivot_inv, col_right).astype(jnp.bfloat16)
    panel_all = jnp.concatenate([col_left, pivot_right], axis=-1)
    slot_ids = jnp.arange(NNEAR, dtype=jnp.int32)
    offsets = slot_ids // NNEAR_DEV * CB_DEV
    global_cols = (near_cols + offsets[None, :]).astype(jnp.int32)

    def one_row(row_items):
        return row_update(row_items[0], pivot_rows, row_items[1], row_items[2], row_items[3], sketch)
    near_new, far_new = lax.map(one_row, (panel_all, target_factors, near_blocks, global_cols))
    return (near_new, far_new)
```

```python
import math

import jax
import jax.numpy as jnp
from jax import lax
from jax.experimental import pallas as pl
from jax.experimental.pallas import tpu as pltpu
from jax.sharding import PartitionSpec as P

F32 = jnp.float32
BF16 = jnp.bfloat16
NN = (((1,), (0,)), ((), ()))
NT = (((1,), (1,)), ((), ()))
TN = (((0,), (0,)), ((), ()))
VMEM_BYTES = 50 * 1024 * 1024


def dot(left, right, dims=NN, precision=None):
    return lax.dot_general(left, right, dims, precision=precision, preferred_element_type=F32)


def halves(shape, half):
    return lax.broadcasted_iota(jnp.int32, shape, len(shape) - 1) // half % 2 == 0


def swap(value, half):
    return jnp.concatenate([value[:, half:], value[:, :half]], axis=1)


def call(kernel, out_shape, in_specs, scratch=(), flops=0, moved=0):
    out_specs = jax.tree.map(lambda _: pl.BlockSpec(memory_space=pltpu.VMEM), out_shape)
    return pl.pallas_call(
        kernel,
        out_shape=out_shape,
        in_specs=in_specs,
        out_specs=out_specs,
        scratch_shapes=list(scratch),
        compiler_params=pltpu.CompilerParams(vmem_limit_bytes=VMEM_BYTES),
        cost_estimate=pl.CostEstimate(flops=flops, bytes_accessed=moved, transcendentals=0),
    )


IN_VMEM = pl.BlockSpec(memory_space=pltpu.VMEM)
IN_SMEM = pl.BlockSpec(memory_space=pltpu.SMEM)
ANYWHERE = pl.BlockSpec(memory_space=pl.ANY)


def pack_rows_kernel(rows_ref, sketch_ref, pb_ref, q_ref):
    _, columns, size, width = rows_ref.shape
    half = width // 2
    for j in range(columns):
        first, second = rows_ref[0, j], rows_ref[1, j]
        lanes = pl.ds(j * width, width)
        pb_ref[:size, lanes] = jnp.concatenate([first[:, :half], second[:, :half]], axis=1)
        q_pair = jnp.concatenate([first[:, half:], second[:, half:]], axis=1)
        q_ref[:, lanes] = q_pair
        pb_ref[pl.ds(size, half), lanes] = dot(sketch_ref[j], q_pair).astype(BF16)


def pack_panel_kernel(panel_ref, inv_ref, out_ref):
    count, pivots, size, width = panel_ref.shape
    half = width // 2
    for k in range(pivots):
        rights = [jnp.transpose(panel_ref[i, k])[half:] for i in range(count)]
        hat = dot(jnp.concatenate(rights, axis=0), inv_ref[k]).astype(BF16)
        for i in range(count):
            start = (k // 2) * count * width + i * width + (k % 2) * half
            out_ref[pl.ds(start, half), :] = hat[i * half : (i + 1) * half]
    base = (pivots // 2) * count * width
    for i in range(count):
        for k in range(0, pivots, 2):
            pair = [panel_ref[i, k + m][:, :half] for m in range(2)]
            out_ref[pl.ds(base + i * size, size), pl.ds(k * half, width)] = jnp.concatenate(pair, axis=1)


def target_sketch_kernel(target_ref, sketch_ref, out_ref):
    count, columns, size, width = target_ref.shape
    half = width // 2
    first = halves((half, width), half)
    zero = jnp.zeros((half, width), BF16)
    for i in range(count):
        for j in range(0, columns, 2):
            core = []
            for m in range(2):
                product = dot(sketch_ref[j + m], target_ref[i, j + m])
                core.append(jnp.where(first, swap(product, half), 0.0).astype(BF16))
            left = jnp.concatenate([target_ref[i, j], target_ref[i, j + 1]], axis=1)
            right = jnp.concatenate(
                [jnp.concatenate([core[0], zero], axis=1), jnp.concatenate([zero, core[1]], axis=1)], axis=0
            )
            out_ref[i, :, pl.ds(j * half, width)] = dot(left, right, NT)


def fetch_all(sources, target, owners_ref, sem):
    copies = []
    for n, source in enumerate(sources):
        copies.append(pltpu.make_async_copy(source, target.at[owners_ref[n]], sem.at[n]))
    for copy in copies:
        copy.start()
    return copies


def sampled_kernel(n_rows, n_cols, row_owner_ref, col_owner_ref, *refs):
    blocks, panels = refs[:n_rows], refs[n_rows : n_rows + n_cols]
    target_ref, mid_ref, sampled_ref, panel_ref, pb_all, weight, sem, sem_panel = refs[n_rows + n_cols :]
    count, size, wide = target_ref.shape
    half = pb_all.shape[1] - size
    width = 2 * half
    columns = wide // half
    copies = fetch_all(blocks, pb_all, row_owner_ref, sem)
    copies += fetch_all(panels, panel_ref, col_owner_ref, sem_panel)
    for copy in copies:
        copy.wait()
    tall = count * width
    row_half = lax.broadcasted_iota(jnp.int32, (tall, 2 * width), 0) // half % 2
    lane_half = lax.broadcasted_iota(jnp.int32, (tall, 2 * width), 1) // half % 2
    same = row_half == lane_half
    zero = jnp.zeros((half, width), BF16)
    per_col = panel_ref.shape[2] // width

    def one_owner(o, carry):
        left = panel_ref[o // per_col, pl.ds(pl.multiple_of(o % per_col * tall, tall), tall), :]
        for j in range(0, columns, 2):
            lanes = pl.ds(j * width, 2 * width)
            mid = dot(left, pb_all[o, :size, lanes])
            mid = jnp.where(same, mid, 0.0).astype(BF16)
            mid_ref[o, :, lanes] = mid
            b_pair = pb_all[o, size:, lanes]
            right = jnp.concatenate(
                [
                    jnp.concatenate([b_pair[:, :width], zero], axis=1),
                    jnp.concatenate([zero, b_pair[:, width:]], axis=1),
                ],
                axis=0,
            )
            product = dot(mid, right, NT).astype(BF16)
            for i in range(count):
                weight[i, pl.ds(pl.multiple_of(o * width, width), width), pl.ds(j * half, width)] = product[
                    i * width : (i + 1) * width
                ]
        return carry

    lax.fori_loop(0, n_rows, one_owner, 0)
    base = per_col * tall
    deep = panel_ref.shape[2]
    for i in range(count):
        total = target_ref[i]
        for c in range(n_cols):
            total = total - dot(panel_ref[c, pl.ds(base + i * size, size), :], weight[i, pl.ds(c * deep, deep), :])
        sampled_ref[i] = total


def basis_kernel(sampled_ref, basis_ref, state):
    count, size, wide = sampled_ref.shape
    _, half, width = state.shape
    columns = wide // half
    pairs = columns // 2
    root_size = math.sqrt(size)
    highest = lax.Precision.HIGHEST
    first = halves((half, width), half)
    lane = lax.broadcasted_iota(jnp.int32, (half, width), 1)
    row = lax.broadcasted_iota(jnp.int32, (half, width), 0)
    n_even = count * pairs
    for i in range(count):
        for p in range(pairs):
            z_pair = sampled_ref[i, :, pl.ds(p * width, width)]
            gram = swap(dot(z_pair, z_pair, TN, highest), half)
            g = i * pairs + p
            state[g] = jnp.where(first, (lane == row).astype(F32), gram[:half])
            state[n_even + g] = jnp.where(first, gram[half:], (lane == row + half).astype(F32))
    sub = 8
    for block in range(half // sub):

        def eliminate(q, carry, block=block):
            pivot = block * sub + q
            below = lax.broadcasted_iota(jnp.int32, (sub, width), 0) > q
            for g in range(2 * n_even):
                offset = half if g < n_even else 0
                index = jnp.full((sub, width), pivot + offset, jnp.int32)
                line = jnp.broadcast_to(state[g, pl.ds(pivot, 1), :], (sub, width))
                top = jnp.take_along_axis(line, index, axis=1)
                line = line / top
                for v in range(block, half // sub):
                    rows = pl.ds(v * sub, sub)
                    tile = state[g, rows, :]
                    column = jnp.take_along_axis(tile, index, axis=1)
                    if v == block:
                        column = jnp.where(below, column, 0.0)
                    state[g, rows, :] = tile - column * line
            return carry

        lax.fori_loop(0, sub, eliminate, 0)
    for i in range(count):
        for p in range(pairs):
            g = i * pairs + p
            even, odd = state[g], state[n_even + g]
            even_diag = jnp.sum(jnp.where(lane == row + half, even, 0.0), axis=1, keepdims=True)
            odd_diag = jnp.sum(jnp.where(lane == row, odd, 0.0), axis=1, keepdims=True)
            even = jnp.where(first, even * (root_size * lax.rsqrt(even_diag)), 0.0)
            odd = jnp.where(first, 0.0, odd * (root_size * lax.rsqrt(odd_diag)))
            inverse = jnp.concatenate([even, odd], axis=0)
            z_pair = sampled_ref[i, :, pl.ds(p * width, width)]
            basis_ref[i, :, pl.ds(p * width, width)] = dot(z_pair, inverse, NT, highest).astype(BF16)


def cores_kernel(n_rows, near_ref, basis_ref, mid_ref, panel_ref, target_ref, left_ref, value_ref, near_left_ref, cores):
    count, size, wide = basis_ref.shape
    columns, width = target_ref.shape[1], target_ref.shape[3]
    half = width // 2
    n_cols, _, deep = panel_ref.shape
    per_col = deep // width
    base = per_col * count * width
    first = halves((half, width), half)
    zero = jnp.zeros((half, width), BF16)
    tall = count * width
    turned = []
    for i in range(count):
        basis_t = jnp.transpose(basis_ref[i])
        turned.append(basis_t)
        for c in range(n_cols):
            cores[i, :, pl.ds(c * deep, deep)] = dot(basis_t, panel_ref[c, pl.ds(base + i * size, size), :]).astype(BF16)
    for i in range(0, count, 2):
        for j in range(columns):
            core = []
            for m in range(2):
                product = dot(turned[i + m][j * half : (j + 1) * half], target_ref[i + m, j])
                core.append(jnp.where(first, 0.0, swap(product, half)).astype(BF16))
            left = jnp.concatenate([target_ref[i, j], target_ref[i + 1, j]], axis=1)
            right = jnp.concatenate(
                [jnp.concatenate([core[0], zero], axis=1), jnp.concatenate([zero, core[1]], axis=1)], axis=0
            )
            value_ref[j, :, pl.ds(i * half, width)] = dot(left, right, NT)

    def one_owner(o, carry):
        lanes = pl.ds(pl.multiple_of(o * width, width), width)
        for i in range(count):
            for j in range(columns):
                product = dot(
                    cores[i, pl.ds(j * half, half), lanes],
                    mid_ref[o, pl.ds(i * width, width), pl.ds(j * width, width)],
                )
                left_ref[j, pl.ds(i * half, half), lanes] = product.astype(BF16)
            near = pl.ds(pl.multiple_of(near_ref[i, 0] * width, width), width)
            x_part = panel_ref[
                o // per_col, pl.ds(base + i * size, size), pl.ds(pl.multiple_of(o % per_col * width, width), width)
            ]
            near_left_ref[i, :, lanes] = dot(x_part, mid_ref[o, pl.ds(i * width, width), near]).astype(BF16)
        return carry

    lax.fori_loop(0, n_rows, one_owner, 0)


def output_kernel(n_rows, near_ref, row_owner_ref, *refs):
    blocks = refs[:n_rows]
    basis_ref, left_ref, value_ref, near_left_ref, near_block_ref, near_out_ref, far_out_ref, q_all, sem = refs[n_rows:]
    count, columns, size, width = far_out_ref.shape
    half = width // 2
    root_size = math.sqrt(size)
    first = halves((size, width), half)
    for copy in fetch_all(blocks, q_all, row_owner_ref, sem):
        copy.wait()
    for j in range(columns):
        right = jnp.concatenate([q_all[o, :, pl.ds(j * width, width)] for o in range(n_rows)], axis=1)
        weights = (value_ref[j] - dot(right, left_ref[j], NT)) / root_size
        for i in range(count):
            tile = weights[:, i // 2 * width : (i // 2 + 1) * width]
            if i % 2 == 0:
                tile = swap(tile, half)
            basis = basis_ref[i, :, pl.ds(j // 2 * width, width)]
            if j % 2 == 1:
                basis = swap(basis, half)
            block = jnp.where(first, basis, tile.astype(BF16))
            is_near = near_ref[i, 0] == j
            for s in range(1, near_ref.shape[1]):
                is_near = jnp.logical_or(is_near, near_ref[i, s] == j)
            far_out_ref[i, j] = jnp.where(is_near, jnp.zeros_like(block), block)
    for i in range(count):
        near = pl.ds(pl.multiple_of(near_ref[i, 0] * width, width), width)
        right = jnp.concatenate([q_all[o, :, near] for o in range(n_rows)], axis=1)
        update = dot(near_left_ref[i], right, NT)
        near_out_ref[i, 0] = (near_block_ref[i, 0].astype(F32) - update).astype(BF16)


def gather_rows(block, after=None):
    n = lax.axis_size("rows")
    me = lax.axis_index("rows")
    if n != 8:
        whole = lax.all_gather(block, "rows")
        return [whole[o] for o in range(n)], jnp.arange(n, dtype=jnp.int32)
    inner = [(2, 4), (4, 2), (3, 5), (5, 3)]
    outward = [(2, 0), (3, 1), (4, 6), (5, 7)]
    exchange = [(i, i ^ 2) for i in range(n)]
    across = [(i, i ^ 1) for i in range(n)]
    send = lambda value, pairs: lax.ppermute(value, "rows", pairs)
    plane = me // 2
    is_end = jnp.logical_or(plane == 0, plane == 3)
    a = send(block, exchange)
    b = send(block, inner)
    x_own = send(block, across)
    c = send(b, outward)
    d = send(a, inner)
    x_a = send(a, across)
    second = jnp.where(is_end, c, b)
    e = send(d, outward)
    x_second = send(second, across)
    third = jnp.where(is_end, e, d)
    x_third = send(third, across)
    low = plane < 2
    near_plane = jnp.where(low, 2, 1) * 2 + me % 2
    far_plane = jnp.where(low, 3, 0) * 2 + me % 2
    owners = jnp.stack([me, me ^ 1, me ^ 2, me ^ 3, near_plane, near_plane ^ 1, far_plane, far_plane ^ 1])
    return [block, x_own, a, x_a, second, x_second, third, x_third], owners.astype(jnp.int32)


def gather_cols(block):
    n = lax.axis_size("cols")
    me = lax.axis_index("cols")
    if n != 4:
        whole = lax.all_gather(block, "cols")
        return [whole[o] for o in range(n)], jnp.arange(n, dtype=jnp.int32)
    core = [(i, i ^ 1) for i in range(n)]
    other = [(i, i ^ 2) for i in range(n)]
    y = lax.ppermute(block, "cols", other)
    own = lax.ppermute(block, "cols", core)
    y_core = lax.ppermute(y, "cols", core)
    owners = jnp.stack([me, me ^ 1, me ^ 2, me ^ 3])
    return [block, own, y, y_core], owners.astype(jnp.int32)


def per_device(panel_cols, pivot_inv, pivot_rows, target_factors, near_blocks, near_cols, sketch):
    n_rows, n_cols = lax.axis_size("rows"), lax.axis_size("cols")
    count, pivots, size, width = panel_cols.shape
    owned, columns = pivot_rows.shape[:2]
    half = width // 2
    wide = columns * half
    assert owned == 2 and columns % 2 == 0 and count % 2 == 0 and pivots % 2 == 0
    assert near_cols.shape[1] == 1
    shape = jax.ShapeDtypeStruct
    sketch_t = jnp.swapaxes(sketch, 1, 2)

    with jax.named_scope("pack_rows"):
        pb, q = call(
            pack_rows_kernel,
            (shape((size + half, columns * width), BF16), shape((size, columns * width), BF16)),
            [IN_VMEM] * 2,
            flops=2 * columns * half * size * width,
            moved=4 * pivot_rows.size,
        )(pivot_rows, sketch_t)
    panel_rows = (pivots // 2) * count * width + count * size
    with jax.named_scope("pack_panel"):
        panel = call(
            pack_panel_kernel,
            shape((panel_rows, pivots * half), BF16),
            [IN_VMEM] * 2,
            flops=2 * count * pivots * half * size * size,
            moved=4 * panel_cols.size,
        )(panel_cols, pivot_inv)
    with jax.named_scope("target_sketch"):
        target_sketch = call(
            target_sketch_kernel,
            shape((count, size, wide), F32),
            [IN_VMEM] * 2,
            flops=4 * target_factors.size * half,
            moved=2 * target_factors.size * 2,
        )(target_factors, sketch_t)

    pb_all, row_owners = gather_rows(pb)
    panels, col_owners = gather_cols(panel)
    q, _ = lax.optimization_barrier((q, pb_all[4]))
    q_all, _ = gather_rows(q)

    vmem = pltpu.VMEM
    with jax.named_scope("sampled"):
        mid, sampled, panel_whole = call(
            lambda *refs: sampled_kernel(n_rows, n_cols, *refs),
            (
                shape((n_rows, count * width, columns * width), BF16),
                shape((count, size, wide), F32),
                shape((n_cols,) + panel.shape, BF16),
            ),
            [IN_SMEM] * 2 + [ANYWHERE] * (n_rows + n_cols) + [IN_VMEM],
            [
                vmem((n_rows,) + pb.shape, BF16),
                vmem((count, n_rows * width, wide), BF16),
                pltpu.SemaphoreType.DMA((n_rows,)),
                pltpu.SemaphoreType.DMA((n_cols,)),
            ],
            flops=8 * n_rows * count * width * size * columns * width // 2,
            moved=2 * n_rows * (pb.size + count * width * columns * width),
        )(row_owners, col_owners, *pb_all, *panels, target_sketch)
    with jax.named_scope("basis"):
        basis = call(
            basis_kernel,
            shape((count, size, wide), BF16),
            [IN_VMEM],
            [vmem((count * columns, half, width), F32)],
            flops=8 * count * columns * half * half * size,
            moved=6 * count * size * wide,
        )(sampled)
    deep = n_rows * width
    with jax.named_scope("cores"):
        left, value, near_left = call(
            lambda *refs: cores_kernel(n_rows, *refs),
            (
                shape((columns, count * half, deep), BF16),
                shape((columns, size, count * half), F32),
                shape((count, size, deep), BF16),
            ),
            [IN_SMEM] + [IN_VMEM] * 4,
            [vmem((count, wide, deep), BF16)],
            flops=6 * n_rows * count * width * size * columns * width // 2,
            moved=2 * n_rows * (pb.size + count * width * columns * width),
        )(near_cols, basis, mid, panel_whole, target_factors)
    with jax.named_scope("output"):
        near_new, far_new = call(
            lambda *refs: output_kernel(n_rows, *refs),
            (shape(near_blocks.shape, BF16), shape(target_factors.shape, BF16)),
            [IN_SMEM] * 2 + [ANYWHERE] * n_rows + [IN_VMEM] * 5,
            [vmem((n_rows,) + q.shape, BF16), pltpu.SemaphoreType.DMA((n_rows,))],
            flops=2 * columns * size * deep * count * half,
            moved=2 * n_rows * q.size,
        )(near_cols, row_owners, *q_all, basis, left, value, near_left, near_blocks)
    return near_new, far_new


def solution(mesh):
    placed = (
        P("rows", "cols", None, None),
        P("cols", None, None),
        P("rows", "cols", None, None),
        P("rows", "cols", None, None),
        P("rows", "cols", None, None),
        P("rows", "cols"),
        P("cols", None, None),
    )
    return jax.shard_map(
        per_device,
        mesh=mesh,
        in_specs=placed,
        out_specs=(P("rows", "cols", None, None), P("rows", "cols", None, None)),
        check_vma=False,
    )
```

```python
import math

import jax
import jax.numpy as jnp
from jax import lax
from jax.experimental import pallas as pl
from jax.experimental.pallas import tpu as pltpu
from jax.sharding import PartitionSpec as P

F32 = jnp.float32
BF16 = jnp.bfloat16
NN = (((1,), (0,)), ((), ()))
NT = (((1,), (1,)), ((), ()))
TN = (((0,), (0,)), ((), ()))
VMEM_BYTES = 50 * 1024 * 1024


def dot(left, right, dims=NN, precision=None):
    return lax.dot_general(left, right, dims, precision=precision, preferred_element_type=F32)


def halves(shape, half):
    return lax.broadcasted_iota(jnp.int32, shape, len(shape) - 1) // half % 2 == 0


def swap(value, half):
    return jnp.concatenate([value[:, half:], value[:, :half]], axis=1)


def call(kernel, out_shape, in_specs, scratch=(), flops=0, moved=0):
    out_specs = jax.tree.map(lambda _: pl.BlockSpec(memory_space=pltpu.VMEM), out_shape)
    return pl.pallas_call(
        kernel,
        out_shape=out_shape,
        in_specs=in_specs,
        out_specs=out_specs,
        scratch_shapes=list(scratch),
        compiler_params=pltpu.CompilerParams(vmem_limit_bytes=VMEM_BYTES),
        cost_estimate=pl.CostEstimate(flops=flops, bytes_accessed=moved, transcendentals=0),
    )


IN_VMEM = pl.BlockSpec(memory_space=pltpu.VMEM)
IN_SMEM = pl.BlockSpec(memory_space=pltpu.SMEM)
ANYWHERE = pl.BlockSpec(memory_space=pl.ANY)


def pack_rows_kernel(rows_ref, sketch_ref, pb_ref, q_ref):
    _, columns, size, width = rows_ref.shape
    half = width // 2
    for j in range(columns):
        first, second = rows_ref[0, j], rows_ref[1, j]
        lanes = pl.ds(j * width, width)
        pb_ref[:size, lanes] = jnp.concatenate([first[:, :half], second[:, :half]], axis=1)
        q_pair = jnp.concatenate([first[:, half:], second[:, half:]], axis=1)
        q_ref[:, lanes] = q_pair
        pb_ref[pl.ds(size, half), lanes] = dot(sketch_ref[j], q_pair).astype(BF16)


def pack_panel_kernel(panel_ref, inv_ref, out_ref):
    count, pivots, size, width = panel_ref.shape
    half = width // 2
    for k in range(pivots):
        rights = [jnp.transpose(panel_ref[i, k])[half:] for i in range(count)]
        hat = dot(jnp.concatenate(rights, axis=0), inv_ref[k]).astype(BF16)
        for i in range(count):
            start = (k // 2) * count * width + i * width + (k % 2) * half
            out_ref[pl.ds(start, half), :] = hat[i * half : (i + 1) * half]
    base = (pivots // 2) * count * width
    for i in range(count):
        for k in range(0, pivots, 2):
            pair = [panel_ref[i, k + m][:, :half] for m in range(2)]
            out_ref[pl.ds(base + i * size, size), pl.ds(k * half, width)] = jnp.concatenate(pair, axis=1)


def target_sketch_kernel(target_ref, sketch_ref, out_ref):
    count, columns, size, width = target_ref.shape
    half = width // 2
    first = halves((half, width), half)
    zero = jnp.zeros((half, width), BF16)
    for i in range(count):
        for j in range(0, columns, 2):
            core = []
            for m in range(2):
                product = dot(sketch_ref[j + m], target_ref[i, j + m])
                core.append(jnp.where(first, swap(product, half), 0.0).astype(BF16))
            left = jnp.concatenate([target_ref[i, j], target_ref[i, j + 1]], axis=1)
            right = jnp.concatenate(
                [jnp.concatenate([core[0], zero], axis=1), jnp.concatenate([zero, core[1]], axis=1)], axis=0
            )
            out_ref[i, :, pl.ds(j * half, width)] = dot(left, right, NT)


def fetch_all(sources, target, owners_ref, sem):
    copies = []
    for n, source in enumerate(sources):
        copies.append(pltpu.make_async_copy(source, target.at[owners_ref[n]], sem.at[n]))
    for copy in copies:
        copy.start()
    return copies


def sampled_kernel(n_rows, n_cols, row_owner_ref, col_owner_ref, *refs):
    blocks, panels = refs[:n_rows], refs[n_rows : n_rows + n_cols]
    target_ref, mid_ref, sampled_ref, panel_ref, pb_all, weight, sem, sem_panel = refs[n_rows + n_cols :]
    count, size, wide = target_ref.shape
    half = pb_all.shape[1] - size
    width = 2 * half
    columns = wide // half
    copies = fetch_all(blocks, pb_all, row_owner_ref, sem)
    copies += fetch_all(panels, panel_ref, col_owner_ref, sem_panel)
    for copy in copies:
        copy.wait()
    tall = count * width
    row_half = lax.broadcasted_iota(jnp.int32, (tall, 2 * width), 0) // half % 2
    lane_half = lax.broadcasted_iota(jnp.int32, (tall, 2 * width), 1) // half % 2
    same = row_half == lane_half
    zero = jnp.zeros((half, width), BF16)
    per_col = panel_ref.shape[2] // width

    def one_owner(o, carry):
        left = panel_ref[o // per_col, pl.ds(pl.multiple_of(o % per_col * tall, tall), tall), :]
        for j in range(0, columns, 2):
            lanes = pl.ds(j * width, 2 * width)
            mid = dot(left, pb_all[o, :size, lanes])
            mid = jnp.where(same, mid, 0.0).astype(BF16)
            mid_ref[o, :, lanes] = mid
            b_pair = pb_all[o, size:, lanes]
            right = jnp.concatenate(
                [
                    jnp.concatenate([b_pair[:, :width], zero], axis=1),
                    jnp.concatenate([zero, b_pair[:, width:]], axis=1),
                ],
                axis=0,
            )
            product = dot(mid, right, NT).astype(BF16)
            for i in range(count):
                weight[i, pl.ds(pl.multiple_of(o * width, width), width), pl.ds(j * half, width)] = product[
                    i * width : (i + 1) * width
                ]
        return carry

    lax.fori_loop(0, n_rows, one_owner, 0)
    base = per_col * tall
    deep = panel_ref.shape[2]
    for i in range(count):
        total = target_ref[i]
        for c in range(n_cols):
            total = total - dot(panel_ref[c, pl.ds(base + i * size, size), :], weight[i, pl.ds(c * deep, deep), :])
        sampled_ref[i] = total


def basis_kernel(sampled_ref, basis_ref, state):
    count, size, wide = sampled_ref.shape
    _, half, width = state.shape
    columns = wide // half
    pairs = columns // 2
    root_size = math.sqrt(size)
    highest = lax.Precision.HIGHEST
    first = halves((half, width), half)
    lane = lax.broadcasted_iota(jnp.int32, (half, width), 1)
    row = lax.broadcasted_iota(jnp.int32, (half, width), 0)
    n_even = count * pairs
    for i in range(count):
        for p in range(pairs):
            z_pair = sampled_ref[i, :, pl.ds(p * width, width)]
            gram = swap(dot(z_pair, z_pair, TN, highest), half)
            g = i * pairs + p
            state[g] = jnp.where(first, (lane == row).astype(F32), gram[:half])
            state[n_even + g] = jnp.where(first, gram[half:], (lane == row + half).astype(F32))
    sub = 8
    total = 2 * n_even
    offsets = [half if g < n_even else 0 for g in range(total)]
    sublane = lax.broadcasted_iota(jnp.int32, (sub, width), 0)

    def pick(tile, index):
        return jnp.take_along_axis(tile, index, axis=1)

    def spread(tile, q):
        return jnp.broadcast_to(tile[q : q + 1], (sub, width))

    def one_block(block, carry):
        start = pl.multiple_of(block * sub, sub)
        tiles = [state[g, pl.ds(start, sub), :] for g in range(total)]

        def lanes_of(q):
            index = jnp.full((sub, width), start + q, jnp.int32)
            return {0: index, half: index + half}

        for q in range(sub - 1):
            index = lanes_of(q)
            columns_q = [pick(tile, index[off]) for tile, off in zip(tiles, offsets)]
            lines = [spread(tile, q) / spread(column, q) for tile, column in zip(tiles, columns_q)]
            below = sublane > q
            tiles = [
                tile - jnp.where(below, column, 0.0) * line for tile, column, line in zip(tiles, columns_q, lines)
            ]
        on_diag = {off: start + off + sublane for off in (0, half)}
        scaled = []
        for g in range(total):
            state[g, pl.ds(start, sub), :] = tiles[g]
            scaled.append(tiles[g] / pick(tiles[g], on_diag[offsets[g]]))

        def update(v, inner):
            rows = pl.ds(pl.multiple_of(v * sub, sub), sub)
            below_tiles = [state[g, rows, :] for g in range(total)]
            for q in range(sub):
                index = lanes_of(q)
                below_tiles = [
                    tile - pick(tile, index[off]) * spread(line, q)
                    for tile, off, line in zip(below_tiles, offsets, scaled)
                ]
            for g in range(total):
                state[g, rows, :] = below_tiles[g]
            return inner

        lax.fori_loop(block + 1, half // sub, update, 0)
        return carry

    lax.fori_loop(0, half // sub, one_block, 0)
    for i in range(count):
        for p in range(pairs):
            g = i * pairs + p
            even, odd = state[g], state[n_even + g]
            even_diag = jnp.sum(jnp.where(lane == row + half, even, 0.0), axis=1, keepdims=True)
            odd_diag = jnp.sum(jnp.where(lane == row, odd, 0.0), axis=1, keepdims=True)
            even = jnp.where(first, even * (root_size * lax.rsqrt(even_diag)), 0.0)
            odd = jnp.where(first, 0.0, odd * (root_size * lax.rsqrt(odd_diag)))
            inverse = jnp.concatenate([even, odd], axis=0)
            z_pair = sampled_ref[i, :, pl.ds(p * width, width)]
            basis_ref[i, :, pl.ds(p * width, width)] = dot(z_pair, inverse, NT, highest).astype(BF16)


def cores_kernel(n_rows, near_ref, basis_ref, mid_ref, panel_ref, target_ref, left_ref, value_ref, near_left_ref, cores):
    count, size, wide = basis_ref.shape
    columns, width = target_ref.shape[1], target_ref.shape[3]
    half = width // 2
    n_cols, _, deep = panel_ref.shape
    per_col = deep // width
    base = per_col * count * width
    first = halves((half, width), half)
    zero = jnp.zeros((half, width), BF16)
    tall = count * width
    turned = []
    for i in range(count):
        basis_t = jnp.transpose(basis_ref[i])
        turned.append(basis_t)
        for c in range(n_cols):
            cores[i, :, pl.ds(c * deep, deep)] = dot(basis_t, panel_ref[c, pl.ds(base + i * size, size), :]).astype(BF16)
    for i in range(0, count, 2):
        for j in range(columns):
            core = []
            for m in range(2):
                product = dot(turned[i + m][j * half : (j + 1) * half], target_ref[i + m, j])
                core.append(jnp.where(first, 0.0, swap(product, half)).astype(BF16))
            left = jnp.concatenate([target_ref[i, j], target_ref[i + 1, j]], axis=1)
            right = jnp.concatenate(
                [jnp.concatenate([core[0], zero], axis=1), jnp.concatenate([zero, core[1]], axis=1)], axis=0
            )
            value_ref[j, :, pl.ds(i * half, width)] = dot(left, right, NT)

    def one_owner(o, carry):
        lanes = pl.ds(pl.multiple_of(o * width, width), width)
        for i in range(count):
            for j in range(columns):
                product = dot(
                    cores[i, pl.ds(j * half, half), lanes],
                    mid_ref[o, pl.ds(i * width, width), pl.ds(j * width, width)],
                )
                left_ref[j, pl.ds(i * half, half), lanes] = product.astype(BF16)
            near = pl.ds(pl.multiple_of(near_ref[i, 0] * width, width), width)
            x_part = panel_ref[
                o // per_col, pl.ds(base + i * size, size), pl.ds(pl.multiple_of(o % per_col * width, width), width)
            ]
            near_left_ref[i, :, lanes] = dot(x_part, mid_ref[o, pl.ds(i * width, width), near]).astype(BF16)
        return carry

    lax.fori_loop(0, n_rows, one_owner, 0)


def output_kernel(n_rows, near_ref, row_owner_ref, *refs):
    blocks = refs[:n_rows]
    basis_ref, left_ref, value_ref, near_left_ref, near_block_ref, near_out_ref, far_out_ref, q_all, sem = refs[n_rows:]
    count, columns, size, width = far_out_ref.shape
    half = width // 2
    root_size = math.sqrt(size)
    first = halves((size, width), half)
    for copy in fetch_all(blocks, q_all, row_owner_ref, sem):
        copy.wait()
    for j in range(columns):
        right = jnp.concatenate([q_all[o, :, pl.ds(j * width, width)] for o in range(n_rows)], axis=1)
        weights = (value_ref[j] - dot(right, left_ref[j], NT)) / root_size
        for i in range(count):
            tile = weights[:, i // 2 * width : (i // 2 + 1) * width]
            if i % 2 == 0:
                tile = swap(tile, half)
            basis = basis_ref[i, :, pl.ds(j // 2 * width, width)]
            if j % 2 == 1:
                basis = swap(basis, half)
            block = jnp.where(first, basis, tile.astype(BF16))
            is_near = near_ref[i, 0] == j
            for s in range(1, near_ref.shape[1]):
                is_near = jnp.logical_or(is_near, near_ref[i, s] == j)
            far_out_ref[i, j] = jnp.where(is_near, jnp.zeros_like(block), block)
    for i in range(count):
        near = pl.ds(pl.multiple_of(near_ref[i, 0] * width, width), width)
        right = jnp.concatenate([q_all[o, :, near] for o in range(n_rows)], axis=1)
        update = dot(near_left_ref[i], right, NT)
        near_out_ref[i, 0] = (near_block_ref[i, 0].astype(F32) - update).astype(BF16)


def gather_rows(block, after=None):
    n = lax.axis_size("rows")
    me = lax.axis_index("rows")
    if n != 8:
        whole = lax.all_gather(block, "rows")
        return [whole[o] for o in range(n)], jnp.arange(n, dtype=jnp.int32)
    inner = [(2, 4), (4, 2), (3, 5), (5, 3)]
    outward = [(2, 0), (3, 1), (4, 6), (5, 7)]
    exchange = [(i, i ^ 2) for i in range(n)]
    across = [(i, i ^ 1) for i in range(n)]
    send = lambda value, pairs: lax.ppermute(value, "rows", pairs)
    plane = me // 2
    is_end = jnp.logical_or(plane == 0, plane == 3)
    a = send(block, exchange)
    b = send(block, inner)
    x_own = send(block, across)
    c = send(b, outward)
    d = send(a, inner)
    x_a = send(a, across)
    second = jnp.where(is_end, c, b)
    e = send(d, outward)
    x_second = send(second, across)
    third = jnp.where(is_end, e, d)
    x_third = send(third, across)
    low = plane < 2
    near_plane = jnp.where(low, 2, 1) * 2 + me % 2
    far_plane = jnp.where(low, 3, 0) * 2 + me % 2
    owners = jnp.stack([me, me ^ 1, me ^ 2, me ^ 3, near_plane, near_plane ^ 1, far_plane, far_plane ^ 1])
    return [block, x_own, a, x_a, second, x_second, third, x_third], owners.astype(jnp.int32)


def gather_cols(block):
    n = lax.axis_size("cols")
    me = lax.axis_index("cols")
    if n != 4:
        whole = lax.all_gather(block, "cols")
        return [whole[o] for o in range(n)], jnp.arange(n, dtype=jnp.int32)
    core = [(i, i ^ 1) for i in range(n)]
    other = [(i, i ^ 2) for i in range(n)]
    y = lax.ppermute(block, "cols", other)
    own = lax.ppermute(block, "cols", core)
    y_core = lax.ppermute(y, "cols", core)
    owners = jnp.stack([me, me ^ 1, me ^ 2, me ^ 3])
    return [block, own, y, y_core], owners.astype(jnp.int32)


def per_device(panel_cols, pivot_inv, pivot_rows, target_factors, near_blocks, near_cols, sketch):
    n_rows, n_cols = lax.axis_size("rows"), lax.axis_size("cols")
    count, pivots, size, width = panel_cols.shape
    owned, columns = pivot_rows.shape[:2]
    half = width // 2
    wide = columns * half
    assert owned == 2 and columns % 2 == 0 and count % 2 == 0 and pivots % 2 == 0
    assert near_cols.shape[1] == 1
    shape = jax.ShapeDtypeStruct
    sketch_t = jnp.swapaxes(sketch, 1, 2)

    with jax.named_scope("pack_rows"):
        pb, q = call(
            pack_rows_kernel,
            (shape((size + half, columns * width), BF16), shape((size, columns * width), BF16)),
            [IN_VMEM] * 2,
            flops=2 * columns * half * size * width,
            moved=4 * pivot_rows.size,
        )(pivot_rows, sketch_t)
    panel_rows = (pivots // 2) * count * width + count * size
    with jax.named_scope("pack_panel"):
        panel = call(
            pack_panel_kernel,
            shape((panel_rows, pivots * half), BF16),
            [IN_VMEM] * 2,
            flops=2 * count * pivots * half * size * size,
            moved=4 * panel_cols.size,
        )(panel_cols, pivot_inv)
    with jax.named_scope("target_sketch"):
        target_sketch = call(
            target_sketch_kernel,
            shape((count, size, wide), F32),
            [IN_VMEM] * 2,
            flops=4 * target_factors.size * half,
            moved=2 * target_factors.size * 2,
        )(target_factors, sketch_t)

    pb_all, row_owners = gather_rows(pb)
    panels, col_owners = gather_cols(panel)
    q, _ = lax.optimization_barrier((q, pb_all[4]))
    q_all, _ = gather_rows(q)

    vmem = pltpu.VMEM
    with jax.named_scope("sampled"):
        mid, sampled, panel_whole = call(
            lambda *refs: sampled_kernel(n_rows, n_cols, *refs),
            (
                shape((n_rows, count * width, columns * width), BF16),
                shape((count, size, wide), F32),
                shape((n_cols,) + panel.shape, BF16),
            ),
            [IN_SMEM] * 2 + [ANYWHERE] * (n_rows + n_cols) + [IN_VMEM],
            [
                vmem((n_rows,) + pb.shape, BF16),
                vmem((count, n_rows * width, wide), BF16),
                pltpu.SemaphoreType.DMA((n_rows,)),
                pltpu.SemaphoreType.DMA((n_cols,)),
            ],
            flops=8 * n_rows * count * width * size * columns * width // 2,
            moved=2 * n_rows * (pb.size + count * width * columns * width),
        )(row_owners, col_owners, *pb_all, *panels, target_sketch)
    with jax.named_scope("basis"):
        basis = call(
            basis_kernel,
            shape((count, size, wide), BF16),
            [IN_VMEM],
            [vmem((count * columns, half, width), F32)],
            flops=8 * count * columns * half * half * size,
            moved=6 * count * size * wide,
        )(sampled)
    deep = n_rows * width
    with jax.named_scope("cores"):
        left, value, near_left = call(
            lambda *refs: cores_kernel(n_rows, *refs),
            (
                shape((columns, count * half, deep), BF16),
                shape((columns, size, count * half), F32),
                shape((count, size, deep), BF16),
            ),
            [IN_SMEM] + [IN_VMEM] * 4,
            [vmem((count, wide, deep), BF16)],
            flops=6 * n_rows * count * width * size * columns * width // 2,
            moved=2 * n_rows * (pb.size + count * width * columns * width),
        )(near_cols, basis, mid, panel_whole, target_factors)
    with jax.named_scope("output"):
        near_new, far_new = call(
            lambda *refs: output_kernel(n_rows, *refs),
            (shape(near_blocks.shape, BF16), shape(target_factors.shape, BF16)),
            [IN_SMEM] * 2 + [ANYWHERE] * n_rows + [IN_VMEM] * 5,
            [vmem((n_rows,) + q.shape, BF16), pltpu.SemaphoreType.DMA((n_rows,))],
            flops=2 * columns * size * deep * count * half,
            moved=2 * n_rows * q.size,
        )(near_cols, row_owners, *q_all, basis, left, value, near_left, near_blocks)
    return near_new, far_new


def solution(mesh):
    placed = (
        P("rows", "cols", None, None),
        P("cols", None, None),
        P("rows", "cols", None, None),
        P("rows", "cols", None, None),
        P("rows", "cols", None, None),
        P("rows", "cols"),
        P("cols", None, None),
    )
    return jax.shard_map(
        per_device,
        mesh=mesh,
        in_specs=placed,
        out_specs=(P("rows", "cols", None, None), P("rows", "cols", None, None)),
        check_vma=False,
    )
```

```python
import math

import jax
import jax.numpy as jnp
from jax import lax
from jax.experimental import pallas as pl
from jax.experimental.pallas import tpu as pltpu
from jax.sharding import PartitionSpec as P

F32 = jnp.float32
BF16 = jnp.bfloat16
NN = (((1,), (0,)), ((), ()))
NT = (((1,), (1,)), ((), ()))
TN = (((0,), (0,)), ((), ()))
PLACE_P = 10
PLACE_Q = 8
VMEM_BYTES = 20 * 1024 * 1024


def dot(left, right, dims=NN, precision=None):
    return lax.dot_general(left, right, dims, precision=precision, preferred_element_type=F32)


def halves(shape, half):
    return lax.broadcasted_iota(jnp.int32, shape, len(shape) - 1) // half % 2 == 0


def swap(value, half):
    return jnp.concatenate([value[:, half:], value[:, :half]], axis=1)


def call(kernel, out_shape, in_specs, scratch=(), flops=0, moved=0):
    out_specs = jax.tree.map(lambda _: pl.BlockSpec(memory_space=pltpu.VMEM), out_shape)
    return pl.pallas_call(
        kernel,
        out_shape=out_shape,
        in_specs=in_specs,
        out_specs=out_specs,
        scratch_shapes=list(scratch),
        compiler_params=pltpu.CompilerParams(vmem_limit_bytes=VMEM_BYTES),
        cost_estimate=pl.CostEstimate(flops=flops, bytes_accessed=moved, transcendentals=0),
    )


IN_VMEM = pl.BlockSpec(memory_space=pltpu.VMEM)
IN_SMEM = pl.BlockSpec(memory_space=pltpu.SMEM)
ANYWHERE = pl.BlockSpec(memory_space=pl.ANY)


def pack_rows_kernel(rows_ref, sketch_ref, pb_ref, q_ref):
    _, columns, size, width = rows_ref.shape
    half = width // 2
    for j in range(columns):
        first, second = rows_ref[0, j], rows_ref[1, j]
        lanes = pl.ds(j * width, width)
        pb_ref[:size, lanes] = jnp.concatenate([first[:, :half], second[:, :half]], axis=1)
        q_pair = jnp.concatenate([first[:, half:], second[:, half:]], axis=1)
        q_ref[:, lanes] = q_pair
        pb_ref[pl.ds(size, half), lanes] = dot(sketch_ref[j], q_pair).astype(BF16)


def pack_panel_kernel(panel_ref, inv_ref, out_ref):
    count, pivots, size, width = panel_ref.shape
    half = width // 2
    for k in range(pivots):
        rights = [jnp.transpose(panel_ref[i, k])[half:] for i in range(count)]
        hat = dot(jnp.concatenate(rights, axis=0), inv_ref[k]).astype(BF16)
        for i in range(count):
            start = (k // 2) * count * width + i * width + (k % 2) * half
            out_ref[pl.ds(start, half), :] = hat[i * half : (i + 1) * half]
    base = (pivots // 2) * count * width
    for i in range(count):
        for k in range(0, pivots, 2):
            pair = [panel_ref[i, k + m][:, :half] for m in range(2)]
            out_ref[pl.ds(base + i * size, size), pl.ds(k * half, width)] = jnp.concatenate(pair, axis=1)


def target_sketch_kernel(target_ref, sketch_ref, out_ref):
    count, columns, size, width = target_ref.shape
    half = width // 2
    first = halves((half, width), half)
    zero = jnp.zeros((half, width), BF16)
    for i in range(count):
        for j in range(0, columns, 2):
            core = []
            for m in range(2):
                product = dot(sketch_ref[j + m], target_ref[i, j + m])
                core.append(jnp.where(first, swap(product, half), 0.0).astype(BF16))
            left = jnp.concatenate([target_ref[i, j], target_ref[i, j + 1]], axis=1)
            right = jnp.concatenate(
                [jnp.concatenate([core[0], zero], axis=1), jnp.concatenate([zero, core[1]], axis=1)], axis=0
            )
            out_ref[i, :, pl.ds(j * half, width)] = dot(left, right, NT)


def fetch_all(sources, target, owners_ref, sem):
    copies = []
    for n, source in enumerate(sources):
        copies.append(pltpu.make_async_copy(source, target.at[owners_ref[n]], sem.at[n]))
    for copy in copies:
        copy.start()
    return copies


def sampled_kernel(n_rows, n_cols, col_owner_ref, pb_all, *refs):
    panels = refs[:n_cols]
    target_ref, mid_ref, sampled_ref, panel_ref, weight, sem_panel = refs[n_cols:]
    count, size, wide = target_ref.shape
    half = pb_all.shape[1] - size
    width = 2 * half
    columns = wide // half
    copies = fetch_all(panels, panel_ref, col_owner_ref, sem_panel)
    for copy in copies:
        copy.wait()
    tall = count * width
    row_half = lax.broadcasted_iota(jnp.int32, (tall, 2 * width), 0) // half % 2
    lane_half = lax.broadcasted_iota(jnp.int32, (tall, 2 * width), 1) // half % 2
    same = row_half == lane_half
    zero = jnp.zeros((half, width), BF16)
    per_col = panel_ref.shape[2] // width

    def one_owner(o, carry):
        left = panel_ref[o // per_col, pl.ds(pl.multiple_of(o % per_col * tall, tall), tall), :]
        for j in range(0, columns, 2):
            lanes = pl.ds(j * width, 2 * width)
            mid = dot(left, pb_all[o, :size, lanes])
            mid = jnp.where(same, mid, 0.0).astype(BF16)
            mid_ref[o, :, lanes] = mid
            b_pair = pb_all[o, size:, lanes]
            right = jnp.concatenate(
                [
                    jnp.concatenate([b_pair[:, :width], zero], axis=1),
                    jnp.concatenate([zero, b_pair[:, width:]], axis=1),
                ],
                axis=0,
            )
            product = dot(mid, right, NT).astype(BF16)
            for i in range(count):
                weight[i, pl.ds(pl.multiple_of(o * width, width), width), pl.ds(j * half, width)] = product[
                    i * width : (i + 1) * width
                ]
        return carry

    lax.fori_loop(0, n_rows, one_owner, 0)
    base = per_col * tall
    deep = panel_ref.shape[2]
    for i in range(count):
        total = target_ref[i]
        for c in range(n_cols):
            total = total - dot(panel_ref[c, pl.ds(base + i * size, size), :], weight[i, pl.ds(c * deep, deep), :])
        sampled_ref[i] = total


def basis_kernel(sampled_ref, basis_ref, state):
    count, size, wide = sampled_ref.shape
    half, held, width = state.shape
    pairs = wide // width
    root_size = math.sqrt(size)
    highest = lax.Precision.HIGHEST
    first = halves((half, width), half)
    for i in range(count):
        for p in range(pairs):
            z_pair = sampled_ref[i, :, pl.ds(p * width, width)]
            gram = dot(z_pair, z_pair, TN, highest)
            state[:, i * pairs + p, :] = jnp.where(first, gram[:half], gram[half:])
    sub = 8
    lane = lax.broadcasted_iota(jnp.int32, (held, width), 1)
    column = lane % half
    origin = lane - column

    def pick(row, pivot):
        return jnp.take_along_axis(row, origin + pivot, axis=1)

    def one_block(block, carry):
        start = block * sub
        rows = [state[start + r] for r in range(sub)]
        core = {(r, s): pick(rows[r], start + s) for r in range(sub) for s in range(r, sub)}
        lines, finals = [], []
        for q in range(sub):
            pivot = start + q
            root = lax.rsqrt(core[q, q])
            inverse = root * root
            finals.append(rows[q])
            unit = jnp.where(column == pivot, 1.0, rows[q])
            state[pivot] = jnp.where(column <= pivot, unit * (root_size * root), 0.0)
            line = unit * inverse
            lines.append(jnp.where(jnp.logical_and(column > pivot, column < start + sub), 0.0, line))
            for r in range(q + 1, sub):
                scaled = core[q, r] * inverse
                rows[r] = jnp.where(column == pivot, 0.0, rows[r]) - core[q, r] * line
                for s in range(r, sub):
                    core[r, s] = core[r, s] - scaled * core[q, s]
        inside = jnp.logical_and(column >= start, column < start + sub)

        def update(v, inner):
            for r in range(sub):
                row = v * sub + r
                value = jnp.where(inside, 0.0, state[row])
                for q in range(sub):
                    value = value - pick(finals[q], row) * lines[q]
                state[row] = value
            return inner

        lax.fori_loop(block + 1, half // sub, update, 0)
        return carry

    lax.fori_loop(0, half // sub, one_block, 0)
    for i in range(count):
        for p in range(pairs):
            inverse = state[:, i * pairs + p, :]
            inverse = jnp.concatenate([jnp.where(first, inverse, 0.0), jnp.where(first, 0.0, inverse)], axis=0)
            z_pair = sampled_ref[i, :, pl.ds(p * width, width)]
            basis_ref[i, :, pl.ds(p * width, width)] = dot(z_pair, inverse, NT, highest).astype(BF16)


def cores_kernel(n_rows, near_ref, basis_ref, mid_ref, panel_ref, target_ref, left_ref, value_ref, near_left_ref, cores):
    count, size, wide = basis_ref.shape
    columns, width = target_ref.shape[1], target_ref.shape[3]
    half = width // 2
    n_cols, _, deep = panel_ref.shape
    per_col = deep // width
    base = per_col * count * width
    first = halves((half, width), half)
    zero = jnp.zeros((half, width), BF16)
    tall = count * width
    turned = []
    for i in range(count):
        basis_t = jnp.transpose(basis_ref[i])
        turned.append(basis_t)
        for c in range(n_cols):
            cores[i, :, pl.ds(c * deep, deep)] = dot(basis_t, panel_ref[c, pl.ds(base + i * size, size), :]).astype(BF16)
    for i in range(0, count, 2):
        for j in range(columns):
            core = []
            for m in range(2):
                product = dot(turned[i + m][j * half : (j + 1) * half], target_ref[i + m, j])
                core.append(jnp.where(first, 0.0, swap(product, half)).astype(BF16))
            left = jnp.concatenate([target_ref[i, j], target_ref[i + 1, j]], axis=1)
            right = jnp.concatenate(
                [jnp.concatenate([core[0], zero], axis=1), jnp.concatenate([zero, core[1]], axis=1)], axis=0
            )
            value_ref[j, :, pl.ds(i * half, width)] = dot(left, right, NT)

    def one_owner(o, carry):
        lanes = pl.ds(pl.multiple_of(o * width, width), width)
        for i in range(count):
            for j in range(columns):
                product = dot(
                    cores[i, pl.ds(j * half, half), lanes],
                    mid_ref[o, pl.ds(i * width, width), pl.ds(j * width, width)],
                )
                left_ref[j, pl.ds(i * half, half), lanes] = product.astype(BF16)
            near = pl.ds(pl.multiple_of(near_ref[i, 0] * width, width), width)
            x_part = panel_ref[
                o // per_col, pl.ds(base + i * size, size), pl.ds(pl.multiple_of(o % per_col * width, width), width)
            ]
            near_left_ref[i, :, lanes] = dot(x_part, mid_ref[o, pl.ds(i * width, width), near]).astype(BF16)
        return carry

    lax.fori_loop(0, n_rows, one_owner, 0)


def output_kernel(n_rows, near_ref, q_all, *refs):
    basis_ref, left_ref, value_ref, near_left_ref, near_block_ref, near_out_ref, far_out_ref = refs
    count, columns, size, width = far_out_ref.shape
    half = width // 2
    root_size = math.sqrt(size)
    first = halves((size, width), half)
    for j in range(columns):
        right = jnp.concatenate([q_all[o, :, pl.ds(j * width, width)] for o in range(n_rows)], axis=1)
        weights = (value_ref[j] - dot(right, left_ref[j], NT)) / root_size
        for i in range(count):
            tile = weights[:, i // 2 * width : (i // 2 + 1) * width]
            if i % 2 == 0:
                tile = swap(tile, half)
            basis = basis_ref[i, :, pl.ds(j // 2 * width, width)]
            if j % 2 == 1:
                basis = swap(basis, half)
            block = jnp.where(first, basis, tile.astype(BF16))
            is_near = near_ref[i, 0] == j
            for s in range(1, near_ref.shape[1]):
                is_near = jnp.logical_or(is_near, near_ref[i, s] == j)
            far_out_ref[i, j] = jnp.where(is_near, jnp.zeros_like(block), block)
    for i in range(count):
        near = pl.ds(pl.multiple_of(near_ref[i, 0] * width, width), width)
        right = jnp.concatenate([q_all[o, :, near] for o in range(n_rows)], axis=1)
        update = dot(near_left_ref[i], right, NT)
        near_out_ref[i, 0] = (near_block_ref[i, 0].astype(F32) - update).astype(BF16)


def place(buffer, owners, blocks, count, micros):
    n = len(blocks)

    def kernel(*refs):
        sources, target, sem = refs[:n], refs[-2], refs[-1]
        copies = fetch_all(sources, target, owners(lax.axis_index("rows")), sem)
        for copy in copies:
            copy.wait()

    held = [] if buffer is None else [buffer]
    return pl.pallas_call(
        kernel,
        out_shape=jax.ShapeDtypeStruct((count,) + blocks[0].shape, blocks[0].dtype),
        in_specs=[IN_VMEM] * (n + len(held)),
        out_specs=IN_VMEM,
        scratch_shapes=[pltpu.SemaphoreType.DMA((n,))],
        input_output_aliases={n: 0} if held else {},
        compiler_params=pltpu.CompilerParams(vmem_limit_bytes=1024 * 1024),
        cost_estimate=pl.CostEstimate(flops=int(micros * 1.15e9), bytes_accessed=0, transcendentals=0),
    )(*blocks, *held)


def gather_rows(block, micros, after=None):
    n = lax.axis_size("rows")
    me = lax.axis_index("rows")
    if n != 8:
        gathered = lax.all_gather(block, "rows")
        return gathered, (block, block), [gathered] * 4
    inner = [(2, 4), (4, 2), (3, 5), (5, 3)]
    outward = [(2, 0), (3, 1), (4, 6), (5, 7)]
    exchange = [(i, i ^ 2) for i in range(n)]
    across = [(i, i ^ 1) for i in range(n)]
    send = lambda value, pairs: lax.ppermute(value, "rows", pairs)
    plane = me // 2
    is_end = jnp.logical_or(plane == 0, plane == 3)
    pair = lambda owner: (owner, owner + 1 - 2 * (owner % 2))
    zy = lambda plane, d: pair(plane * 2 + d % 2)
    a = send(block, exchange)
    b = send(block, inner)
    if after is not None:
        block, _ = lax.optimization_barrier((block, after))
    x_own = send(block, across)
    stages = [place(None, pair, [block, x_own], n, micros)]
    c = send(b, outward)
    d = send(a, inner)
    x_a = send(a, across)
    stages.append(place(stages[-1], lambda d: zy(d // 2 + 1 - 2 * (d // 2 % 2), d), [a, x_a], n, micros))
    second = jnp.where(is_end, c, b)
    e = send(d, outward)
    x_second = send(second, across)
    stages.append(place(stages[-1], lambda d: zy(jnp.where(d < 4, 2, 1), d), [second, x_second], n, micros))
    third = jnp.where(is_end, e, d)
    x_third = send(third, across)
    stages.append(place(stages[-1], lambda d: zy(jnp.where(d < 4, 3, 0), d), [third, x_third], n, micros))
    return stages[-1], (second, third), stages


def gather_cols(block):
    n = lax.axis_size("cols")
    me = lax.axis_index("cols")
    if n != 4:
        whole = lax.all_gather(block, "cols")
        return [whole[o] for o in range(n)], jnp.arange(n, dtype=jnp.int32)
    core = [(i, i ^ 1) for i in range(n)]
    other = [(i, i ^ 2) for i in range(n)]
    y = lax.ppermute(block, "cols", other)
    own = lax.ppermute(block, "cols", core)
    y_core = lax.ppermute(y, "cols", core)
    owners = jnp.stack([me, me ^ 1, me ^ 2, me ^ 3])
    return [block, own, y, y_core], owners.astype(jnp.int32)


def per_device(panel_cols, pivot_inv, pivot_rows, target_factors, near_blocks, near_cols, sketch):
    n_rows, n_cols = lax.axis_size("rows"), lax.axis_size("cols")
    count, pivots, size, width = panel_cols.shape
    owned, columns = pivot_rows.shape[:2]
    half = width // 2
    wide = columns * half
    assert owned == 2 and columns % 2 == 0 and count % 2 == 0 and pivots % 2 == 0
    assert near_cols.shape[1] == 1
    shape = jax.ShapeDtypeStruct
    sketch_t = jnp.swapaxes(sketch, 1, 2)

    with jax.named_scope("pack_rows"):
        pb, q = call(
            pack_rows_kernel,
            (shape((size + half, columns * width), BF16), shape((size, columns * width), BF16)),
            [IN_VMEM] * 2,
            flops=2 * columns * half * size * width,
            moved=4 * pivot_rows.size,
        )(pivot_rows, sketch_t)
    panel_rows = (pivots // 2) * count * width + count * size
    with jax.named_scope("pack_panel"):
        panel = call(
            pack_panel_kernel,
            shape((panel_rows, pivots * half), BF16),
            [IN_VMEM] * 2,
            flops=2 * count * pivots * half * size * size,
            moved=4 * panel_cols.size,
        )(panel_cols, pivot_inv)
    pb_all, (_, pb_third), _ = gather_rows(pb, PLACE_P)
    panels, col_owners = gather_cols(panel)
    q, target_late, _ = lax.optimization_barrier((q, target_factors, pb_third))
    with jax.named_scope("target_sketch"):
        target_sketch = call(
            target_sketch_kernel,
            shape((count, size, wide), F32),
            [IN_VMEM] * 2,
            flops=4 * target_factors.size * half,
            moved=2 * target_factors.size * 2,
        )(target_late, sketch_t)
    q_all, _, q_stages = gather_rows(q, PLACE_Q, pb_all)

    vmem = pltpu.VMEM
    with jax.named_scope("sampled"):
        mid, sampled, panel_whole = call(
            lambda *refs: sampled_kernel(n_rows, n_cols, *refs),
            (
                shape((n_rows, count * width, columns * width), BF16),
                shape((count, size, wide), F32),
                shape((n_cols,) + panel.shape, BF16),
            ),
            [IN_SMEM, IN_VMEM] + [ANYWHERE] * n_cols + [IN_VMEM],
            [
                vmem((count, n_rows * width, wide), BF16),
                pltpu.SemaphoreType.DMA((n_cols,)),
            ],
            flops=8 * n_rows * count * width * size * columns * width // 2,
            moved=2 * n_rows * (pb.size + count * width * columns * width),
        )(col_owners, pb_all, *panels, target_sketch)
    sampled, _ = lax.optimization_barrier((sampled, q_stages[1]))
    with jax.named_scope("basis"):
        basis = call(
            basis_kernel,
            shape((count, size, wide), BF16),
            [IN_VMEM],
            [vmem((half, -(-count * columns // 2 // 8) * 8, width), F32)],
            flops=8 * count * columns * half * half * size,
            moved=6 * count * size * wide,
        )(sampled)
    deep = n_rows * width
    basis, _ = lax.optimization_barrier((basis, q_stages[2]))
    with jax.named_scope("cores"):
        left, value, near_left = call(
            lambda *refs: cores_kernel(n_rows, *refs),
            (
                shape((columns, count * half, deep), BF16),
                shape((columns, size, count * half), F32),
                shape((count, size, deep), BF16),
            ),
            [IN_SMEM] + [IN_VMEM] * 4,
            [vmem((count, wide, deep), BF16)],
            flops=6 * n_rows * count * width * size * columns * width // 2,
            moved=2 * n_rows * (pb.size + count * width * columns * width),
        )(near_cols, basis, mid, panel_whole, target_factors)
    with jax.named_scope("output"):
        near_new, far_new = call(
            lambda *refs: output_kernel(n_rows, *refs),
            (shape(near_blocks.shape, BF16), shape(target_factors.shape, BF16)),
            [IN_SMEM] + [IN_VMEM] * 6,
            flops=2 * columns * size * deep * count * half,
            moved=2 * n_rows * q.size,
        )(near_cols, q_all, basis, left, value, near_left, near_blocks)
    return near_new, far_new


def solution(mesh):
    placed = (
        P("rows", "cols", None, None),
        P("cols", None, None),
        P("rows", "cols", None, None),
        P("rows", "cols", None, None),
        P("rows", "cols", None, None),
        P("rows", "cols"),
        P("cols", None, None),
    )
    return jax.shard_map(
        per_device,
        mesh=mesh,
        in_specs=placed,
        out_specs=(P("rows", "cols", None, None), P("rows", "cols", None, None)),
        check_vma=False,
    )
```

```python
import math

import jax
import jax.numpy as jnp
from jax import lax
from jax.experimental import pallas as pl
from jax.experimental.pallas import tpu as pltpu
from jax.sharding import PartitionSpec as P

F32 = jnp.float32
BF16 = jnp.bfloat16
NN = (((1,), (0,)), ((), ()))
NT = (((1,), (1,)), ((), ()))
TN = (((0,), (0,)), ((), ()))
PLACE_VMEM = 1024 * 1024
PLACE_P = 10
PLACE_Q = 8
PLACE_Q0 = 1
MID_SCALE = 1
SAMPLED_SCALE = 1
BLOCKS = 3
GRAM_FLOPS = int(1e9)
BETWEEN = "second"
CORES_SCALE = 1
TIE0 = 2
TIE_Y = 1
TIE_GRAM = 0
BASIS_FLOPS = int(1e9)
FORWARD_AT = "gram"
NEAR_AT = "pb"
GATE_ALONG = "third"
GATE_FORWARD = "pb"
TIE1 = "cores"
EARLY_Q = 0
VMEM_BYTES = 14 * 1024 * 1024


def dot(left, right, dims=NN, precision=None):
    return lax.dot_general(left, right, dims, precision=precision, preferred_element_type=F32)


def halves(shape, half):
    return lax.broadcasted_iota(jnp.int32, shape, len(shape) - 1) // half % 2 == 0


def swap(value, half):
    return jnp.concatenate([value[:, half:], value[:, :half]], axis=1)


def call(kernel, out_shape, in_specs, scratch=(), flops=0, moved=0, aliases=None):
    out_specs = jax.tree.map(lambda _: pl.BlockSpec(memory_space=pltpu.VMEM), out_shape)
    return pl.pallas_call(
        kernel,
        out_shape=out_shape,
        in_specs=in_specs,
        out_specs=out_specs,
        scratch_shapes=list(scratch),
        input_output_aliases=aliases or {},
        compiler_params=pltpu.CompilerParams(vmem_limit_bytes=VMEM_BYTES),
        cost_estimate=pl.CostEstimate(flops=flops, bytes_accessed=moved, transcendentals=0),
    )


IN_VMEM = pl.BlockSpec(memory_space=pltpu.VMEM)
IN_SMEM = pl.BlockSpec(memory_space=pltpu.SMEM)
ANYWHERE = pl.BlockSpec(memory_space=pl.ANY)


def pack_rows_kernel(rows_ref, sketch_ref, pb_ref, q_ref):
    _, columns, size, width = rows_ref.shape
    half = width // 2
    for j in range(columns):
        first, second = rows_ref[0, j], rows_ref[1, j]
        lanes = pl.ds(j * width, width)
        pb_ref[:size, lanes] = jnp.concatenate([first[:, :half], second[:, :half]], axis=1)
        q_pair = jnp.concatenate([first[:, half:], second[:, half:]], axis=1)
        q_ref[:, lanes] = q_pair
        pb_ref[pl.ds(size, half), lanes] = dot(sketch_ref[j], q_pair).astype(BF16)


def pack_panel_kernel(panel_ref, inv_ref, out_ref):
    count, pivots, size, width = panel_ref.shape
    half = width // 2
    for k in range(pivots):
        rights = [jnp.transpose(panel_ref[i, k])[half:] for i in range(count)]
        hat = dot(jnp.concatenate(rights, axis=0), inv_ref[k]).astype(BF16)
        for i in range(count):
            start = (k // 2) * count * width + i * width + (k % 2) * half
            out_ref[pl.ds(start, half), :] = hat[i * half : (i + 1) * half]
    base = (pivots // 2) * count * width
    for i in range(count):
        for k in range(0, pivots, 2):
            pair = [panel_ref[i, k + m][:, :half] for m in range(2)]
            out_ref[pl.ds(base + i * size, size), pl.ds(k * half, width)] = jnp.concatenate(pair, axis=1)


def target_sketch(target_ref, sketch_ref, out_ref):
    count, columns, size, width = target_ref.shape
    half = width // 2
    first = halves((half, width), half)
    zero = jnp.zeros((half, width), BF16)
    for i in range(count):
        for j in range(0, columns, 2):
            core = []
            for m in range(2):
                product = dot(sketch_ref[j + m], target_ref[i, j + m])
                core.append(jnp.where(first, swap(product, half), 0.0).astype(BF16))
            left = jnp.concatenate([target_ref[i, j], target_ref[i, j + 1]], axis=1)
            right = jnp.concatenate(
                [jnp.concatenate([core[0], zero], axis=1), jnp.concatenate([zero, core[1]], axis=1)], axis=0
            )
            out_ref[i, :, pl.ds(j * half, width)] = dot(left, right, NT)


def fetch_all(sources, target, owners_ref, sem):
    copies = []
    for n, source in enumerate(sources):
        copies.append(pltpu.make_async_copy(source, target.at[owners_ref[n]], sem.at[n]))
    for copy in copies:
        copy.start()
    return copies


def mid_pair(n_rows, t, pb_all, panel_ref, mid_ref, slot, weight_ref):
    _, tall, wide = mid_ref.shape
    count = weight_ref.shape[0]
    width = tall // count
    half = width // 2
    columns = wide // width
    size = pb_all.shape[1] - half
    row_half = lax.broadcasted_iota(jnp.int32, (tall, 2 * width), 0) // half % 2
    lane_half = lax.broadcasted_iota(jnp.int32, (tall, 2 * width), 1) // half % 2
    same = row_half == lane_half
    zero = jnp.zeros((half, width), BF16)
    first = arrivals(n_rows)(lax.axis_index("rows"), t)
    plane = first // 2
    for m in range(2):
        part = (first + m) % 2
        left = panel_ref[plane, pl.ds(pl.multiple_of(part * tall, tall), tall), :]
        for j in range(0, columns, 2):
            lanes = pl.ds(j * width, 2 * width)
            mid = dot(left, pb_all[t + m, :size, lanes])
            mid = jnp.where(same, mid, 0.0).astype(BF16)
            mid_ref[slot + m, :, lanes] = mid
            b_pair = pb_all[t + m, size:, lanes]
            right = jnp.concatenate(
                [
                    jnp.concatenate([b_pair[:, :width], zero], axis=1),
                    jnp.concatenate([zero, b_pair[:, width:]], axis=1),
                ],
                axis=0,
            )
            product = dot(mid, right, NT).astype(BF16)
            for i in range(count):
                weight_ref[i, pl.ds(pl.multiple_of(part * width, width), width), pl.ds(j * half, width)] = product[
                    i * width : (i + 1) * width
                ]
    return plane


def subtract(total_ref, panel_ref, plane, weight_ref):
    count, size, _ = total_ref.shape
    base = panel_ref.shape[1] - count * size
    for i in range(count):
        total_ref[i] = total_ref[i] - dot(panel_ref[plane, pl.ds(base + i * size, size), :], weight_ref[i])


def mid_kernel(n_rows, n_cols, pb_all, target_ref, sketch_ref, *refs):
    panels = refs[:n_cols]
    mid_ref, total_ref, panel_ref, weight, sem_panel = refs[n_cols:]
    copies = fetch_all(panels, panel_ref, column_owners(n_cols), sem_panel)
    target_sketch(target_ref, sketch_ref, total_ref)
    for copy in copies:
        copy.wait()

    def step(s, carry):
        plane = mid_pair(n_rows, 2 * s, pb_all, panel_ref, mid_ref, 2 * s, weight)
        subtract(total_ref, panel_ref, plane, weight)
        return carry

    lax.fori_loop(0, n_rows // 2 - 1, step, 0)


def sampled_kernel(n_rows, pb_all, panel_ref, total_ref, mid_ref, sampled_ref, weight):
    plane = mid_pair(n_rows, n_rows - 2, pb_all, panel_ref, mid_ref, 0, weight)
    sampled_ref[...] = total_ref[...]
    subtract(sampled_ref, panel_ref, plane, weight)


def gram_kernel(blocks, sampled_ref, state):
    count, _, wide = sampled_ref.shape
    half, _, width = state.shape
    pairs = wide // width
    first = halves((half, width), half)
    for i in range(count):
        for p in range(pairs):
            z_pair = sampled_ref[i, :, pl.ds(p * width, width)]
            gram = dot(z_pair, z_pair, TN, lax.Precision.HIGHEST)
            state[:, i * pairs + p, :] = jnp.where(first, gram[:half], gram[half:])
    eliminate(state, 0, blocks, math.sqrt(sampled_ref.shape[1]))


def basis_kernel(blocks, sampled_ref, state_in, state, basis_ref):
    count, size, wide = sampled_ref.shape
    half, _, width = state.shape
    pairs = wide // width
    first = halves((half, width), half)
    eliminate(state, blocks, half // 8, math.sqrt(size))
    for i in range(count):
        for p in range(pairs):
            inverse = state[:, i * pairs + p, :]
            inverse = jnp.concatenate([jnp.where(first, inverse, 0.0), jnp.where(first, 0.0, inverse)], axis=0)
            z_pair = sampled_ref[i, :, pl.ds(p * width, width)]
            product = dot(z_pair, inverse, NT, lax.Precision.HIGHEST)
            basis_ref[i, :, pl.ds(p * width, width)] = product.astype(BF16)


def eliminate(state, first_block, last_block, root_size):
    half, held, width = state.shape
    sub = 8
    lane = lax.broadcasted_iota(jnp.int32, (held, width), 1)
    column = lane % half
    origin = lane - column

    def pick(row, pivot):
        return jnp.take_along_axis(row, origin + pivot, axis=1)

    def one_block(block, carry):
        start = block * sub
        rows = [state[start + r] for r in range(sub)]
        core = {(r, s): pick(rows[r], start + s) for r in range(sub) for s in range(r, sub)}
        lines, finals = [], []
        for q in range(sub):
            pivot = start + q
            root = lax.rsqrt(core[q, q])
            inverse = root * root
            finals.append(rows[q])
            unit = jnp.where(column == pivot, 1.0, rows[q])
            state[pivot] = jnp.where(column <= pivot, unit * (root_size * root), 0.0)
            line = unit * inverse
            lines.append(jnp.where(jnp.logical_and(column > pivot, column < start + sub), 0.0, line))
            for r in range(q + 1, sub):
                scaled = core[q, r] * inverse
                rows[r] = jnp.where(column == pivot, 0.0, rows[r]) - core[q, r] * line
                for s in range(r, sub):
                    core[r, s] = core[r, s] - scaled * core[q, s]
        inside = jnp.logical_and(column >= start, column < start + sub)

        def update(v, inner):
            for r in range(sub):
                row = v * sub + r
                value = jnp.where(inside, 0.0, state[row])
                for q in range(sub):
                    value = value - pick(finals[q], row) * lines[q]
                state[row] = value
            return inner

        lax.fori_loop(block + 1, half // sub, update, 0)
        return carry

    lax.fori_loop(first_block, last_block, one_block, 0)


def cores_kernel(
    n_rows, near_ref, basis_ref, early_ref, late_ref, panel_ref, target_ref, left_ref, value_ref, near_left_ref, cores
):
    count, size, wide = basis_ref.shape
    columns, width = target_ref.shape[1], target_ref.shape[3]
    half = width // 2
    n_cols, _, deep = panel_ref.shape
    per_col = deep // width
    base = per_col * count * width
    first = halves((half, width), half)
    zero = jnp.zeros((half, width), BF16)
    tall = count * width
    turned = []
    for i in range(count):
        basis_t = jnp.transpose(basis_ref[i])
        turned.append(basis_t)
        for c in range(n_cols):
            cores[i, :, pl.ds(c * deep, deep)] = dot(basis_t, panel_ref[c, pl.ds(base + i * size, size), :]).astype(BF16)
    for i in range(0, count, 2):
        for j in range(columns):
            core = []
            for m in range(2):
                product = dot(turned[i + m][j * half : (j + 1) * half], target_ref[i + m, j])
                core.append(jnp.where(first, 0.0, swap(product, half)).astype(BF16))
            left = jnp.concatenate([target_ref[i, j], target_ref[i + 1, j]], axis=1)
            right = jnp.concatenate(
                [jnp.concatenate([core[0], zero], axis=1), jnp.concatenate([zero, core[1]], axis=1)], axis=0
            )
            value_ref[j, :, pl.ds(i * half, width)] = dot(left, right, NT)

    owner = arrivals(n_rows)
    me = lax.axis_index("rows")

    def one_pair(t, mid_ref, slot):
        o = owner(me, t)
        lanes = pl.ds(pl.multiple_of(t * width, width), width)
        from_lanes = pl.ds(pl.multiple_of(o * width, width), width)
        for i in range(count):
            for j in range(columns):
                product = dot(
                    cores[i, pl.ds(j * half, half), from_lanes],
                    mid_ref[slot, pl.ds(i * width, width), pl.ds(j * width, width)],
                )
                left_ref[j, pl.ds(i * half, half), lanes] = product.astype(BF16)
            near = pl.ds(pl.multiple_of(near_ref[0, i] * width, width), width)
            x_part = panel_ref[
                o // per_col, pl.ds(base + i * size, size), pl.ds(pl.multiple_of(o % per_col * width, width), width)
            ]
            near_left_ref[i, :, lanes] = dot(x_part, mid_ref[slot, pl.ds(i * width, width), near]).astype(BF16)

    def step(t, carry):
        one_pair(t, early_ref, t)
        return carry

    lax.fori_loop(0, n_rows - 2, step, 0)
    for m in range(2):
        one_pair(n_rows - 2 + m, late_ref, m)


def output_kernel(n_rows, near_ref, q_all, *refs):
    basis_ref, left_ref, value_ref, near_left_ref, near_block_ref, near_out_ref, far_out_ref = refs
    count, columns, size, width = far_out_ref.shape
    half = width // 2
    root_size = math.sqrt(size)
    first = halves((size, width), half)
    for j in range(columns):
        right = jnp.concatenate([q_all[o, :, pl.ds(j * width, width)] for o in range(n_rows)], axis=1)
        weights = (value_ref[j] - dot(right, left_ref[j], NT)) / root_size
        for i in range(count):
            tile = weights[:, i // 2 * width : (i // 2 + 1) * width]
            if i % 2 == 0:
                tile = swap(tile, half)
            basis = basis_ref[i, :, pl.ds(j // 2 * width, width)]
            if j % 2 == 1:
                basis = swap(basis, half)
            block = jnp.where(first, basis, tile.astype(BF16))
            is_near = near_ref[0, i] == j
            for s in range(1, near_ref.shape[0]):
                is_near = jnp.logical_or(is_near, near_ref[s, i] == j)
            far_out_ref[i, j] = jnp.where(is_near, jnp.zeros_like(block), block)
    for i in range(count):
        near = pl.ds(pl.multiple_of(near_ref[0, i] * width, width), width)
        right = jnp.concatenate([q_all[o, :, near] for o in range(n_rows)], axis=1)
        update = dot(near_left_ref[i], right, NT)
        near_out_ref[i, 0] = (near_block_ref[i, 0].astype(F32) - update).astype(BF16)


def arrivals(n):
    if n != 8:
        return lambda me, t: t
    third = lambda me: jnp.where(me < 4, 4, 2) + me % 2
    fourth = lambda me: jnp.where(me < 4, 6, 0) + me % 2

    def owner(me, t):
        base = jnp.where(t < 2, me, jnp.where(t < 4, me ^ 2, jnp.where(t < 6, third(me), fourth(me))))
        return base ^ (t % 2)

    return owner


def held(value, *events):
    events = [event for event in events if event is not None]
    return lax.optimization_barrier((value,) + tuple(events))[0] if events else value


def place(buffer, t, blocks, n, micros):
    def kernel(*refs):
        sources, target, sem = refs[:2], refs[-2], refs[-1]
        slot = t(lax.axis_index("rows")) if callable(t) else t
        copies = fetch_all(sources, target, [slot, slot + 1], sem)
        for copy in copies:
            copy.wait()

    given = [] if buffer is None else [buffer]
    return pl.pallas_call(
        kernel,
        out_shape=jax.ShapeDtypeStruct((n,) + blocks[0].shape, blocks[0].dtype),
        in_specs=[IN_VMEM] * (2 + len(given)),
        out_specs=IN_VMEM,
        scratch_shapes=[pltpu.SemaphoreType.DMA((2,))],
        input_output_aliases={2: 0} if given else {},
        compiler_params=pltpu.CompilerParams(vmem_limit_bytes=1024 * 1024),
        cost_estimate=pl.CostEstimate(flops=int(micros * 1.15e9), bytes_accessed=0, transcendentals=0),
    )(*blocks, *given)


class Gather:
    slots = [0, 2, 4, 6]
    inner = [(2, 4), (4, 2), (3, 5), (5, 3)]
    outward = [(2, 0), (3, 1), (4, 6), (5, 7)]

    def __init__(self, block, micros):
        self.n = lax.axis_size("rows")
        self.block, self.micros, self.whole = block, micros, None
        me = lax.axis_index("rows")
        self.is_end = jnp.logical_or(me < 2, me >= self.n - 2)

    def send(self, value, pairs):
        return lax.ppermute(value, "rows", pairs)

    def flip(self, value, bits):
        return self.send(value, [(i, i ^ bits) for i in range(self.n)])

    def start_across(self, *events):
        self.x_own = self.flip(held(self.block, *events), 1)

    def start_along(self, *events):
        block = held(self.block, *events)
        self.near, self.mid = self.flip(block, 2), self.send(block, self.inner)

    def forward(self, *events):
        self.x_near = self.flip(held(self.near, *events), 1)
        self.far = self.send(held(self.near, *events), self.inner)
        out = self.send(held(self.mid, *events), self.outward)
        self.second = jnp.where(self.is_end, out, self.mid)

    def forward_again(self, *events):
        self.x_second = self.flip(held(self.second, *events), 1)
        out = self.send(held(self.far, *events), self.outward)
        self.third = jnp.where(self.is_end, out, self.far)

    def finish(self, *events):
        self.x_third = self.flip(held(self.third, *events), 1)

    def put(self, stage, *events):
        pair = [
            lambda: (self.block, self.x_own),
            lambda: (self.near, self.x_near),
            lambda: (self.second, self.x_second),
            lambda: (self.third, self.x_third),
        ][stage]()
        pair = (pair[0], held(pair[1], *events)) if stage == 0 else pair
        whole = self.whole if stage == 0 or all(event is None for event in events) else held(self.whole, *events)
        self.whole = place(whole, self.slots[stage], pair, self.n, self.micros)
        return self.whole


class DirectGather(Gather):
    slots = [0, 2, lambda me: jnp.where((me < 2) | (me > 5), 4, 6), lambda me: jnp.where((me < 2) | (me > 5), 6, 4)]

    def start_along(self, *events):
        block = held(self.block, *events)
        self.second, self.near = self.flip(block, 4), self.flip(block, 2)

    def exchange_near(self, *events):
        self.x_near = self.flip(held(self.near, *events), 1)

    def forward(self, *events):
        out = self.send(held(self.second, *events), self.outward)
        middle = self.send(held(self.block, self.second, *events), self.inner)
        self.x_second = self.flip(held(self.second, *events), 1)
        self.third = jnp.where(self.is_end, out, middle)


class PlainGather:
    def __init__(self, block, micros):
        self.block = self.near = self.second = self.third = self.far = block
        self.whole = None

    def start_across(self, *events):
        pass

    start_along = forward = forward_again = finish = exchange_near = start_across

    def put(self, stage, *events):
        if self.whole is None:
            self.whole = lax.all_gather(self.block, "rows")
        return self.whole


def column_owners(n):
    me = lax.axis_index("cols")
    return [me ^ t for t in range(n)] if n == 4 else list(range(n))


def gather_cols(block):
    n = lax.axis_size("cols")
    if n != 4:
        whole = lax.all_gather(block, "cols")
        return [whole[o] for o in range(n)]
    core = [(i, i ^ 1) for i in range(n)]
    other = [(i, i ^ 2) for i in range(n)]
    y = lax.ppermute(block, "cols", other)
    own = lax.ppermute(block, "cols", core)
    return [block, own, y, lax.ppermute(y, "cols", core)]


def per_device(panel_cols, pivot_inv, pivot_rows, target_factors, near_blocks, near_cols, sketch):
    n_rows, n_cols = lax.axis_size("rows"), lax.axis_size("cols")
    count, pivots, size, width = panel_cols.shape
    owned, columns = pivot_rows.shape[:2]
    half = width // 2
    wide = columns * half
    assert owned == 2 and columns % 2 == 0 and count % 2 == 0 and pivots % 2 == 0
    assert near_cols.shape[1] == 1
    shape = jax.ShapeDtypeStruct
    sketch_t = jnp.swapaxes(sketch, 1, 2)
    near_t = near_cols.T

    with jax.named_scope("pack_rows"):
        pb, q = call(
            pack_rows_kernel,
            (shape((size + half, columns * width), BF16), shape((size, columns * width), BF16)),
            [IN_VMEM] * 2,
            flops=2 * columns * half * size * width,
            moved=4 * pivot_rows.size,
        )(pivot_rows, sketch_t)
    panel_rows = (pivots // 2) * count * width + count * size
    with jax.named_scope("pack_panel"):
        panel = call(
            pack_panel_kernel,
            shape((panel_rows, pivots * half), BF16),
            [IN_VMEM] * 2,
            flops=2 * count * pivots * half * size * size,
            moved=4 * panel_cols.size,
        )(panel_cols, pivot_inv)
    panels = gather_cols(panel)
    vmem = pltpu.VMEM
    deep = n_rows * width
    mid_flops = 4 * count * width * size * columns * width
    weight_scratch = vmem((count, 2 * width, wide), BF16)

    def mids(arrived, target):
        with jax.named_scope("mid"):
            return call(
                lambda *refs: mid_kernel(n_rows, n_cols, *refs),
                (
                    shape((n_rows - 2, count * width, columns * width), BF16),
                    shape((count, size, wide), F32),
                    shape((n_cols,) + panel.shape, BF16),
                ),
                [IN_VMEM] * 3 + [ANYWHERE] * n_cols,
                [weight_scratch, pltpu.SemaphoreType.DMA((n_cols,))],
                flops=mid_flops * (n_rows - 2) * MID_SCALE,
            )(arrived, target, sketch_t, *panels)

    kind = Gather if n_rows == 8 else PlainGather
    pb_way = kind(pb, PLACE_P)
    q_way = (DirectGather if n_rows == 8 else kind)(q, PLACE_Q)
    pb_way.start_along()
    pb_way.start_across()
    pb_way.forward()
    if TIE0 < 3:
        q_way.start_across(pb_way.near)
    pb_way.forward_again()
    pb_way.finish()
    pb_way.put(0, panels[2] if TIE_Y == 2 else None)
    q_way.micros = PLACE_Q0
    q_first = q_way.put(0) if TIE0 < 3 else None
    pb_way.put(1, q_first if TIE0 == 1 else None, panels[2] if TIE_Y == 1 else None)
    arrived = pb_way.put(2, q_first if TIE0 == 2 else None)
    q_way.micros = PLACE_Q
    mid_early, total, panel_whole = mids(arrived, held(target_factors, pb_way.far))
    if GATE_ALONG == "third":
        q_way.start_along(pb_way.third)
    if GATE_ALONG == "mid":
        q_way.start_along(total)
    if GATE_ALONG == "far":
        q_way.start_along(pb_way.far)
    pb_all = pb_way.put(3, total)
    if TIE0 == 3:
        q_way.start_across(pb_all)
        q_way.put(0)
    with jax.named_scope("sampled"):
        mid_late, sampled = call(
            lambda *refs: sampled_kernel(n_rows, *refs),
            (shape((2,) + mid_early.shape[1:], BF16), shape((count, size, wide), F32)),
            [IN_VMEM] * 3,
            [weight_scratch],
            flops=mid_flops * 2 * SAMPLED_SCALE,
        )(pb_all, panel_whole, total)
    if NEAR_AT != "gram":
        q_way.exchange_near({"pb": pb_all, "sampled": sampled}[NEAR_AT])
    if FORWARD_AT == "pb":
        q_way.forward(pb_all)
    state_shape = shape((half, -(-count * columns // 2 // 8) * 8, width), F32)
    with jax.named_scope("gram"):
        state = call(
            lambda *refs: gram_kernel(BLOCKS, *refs),
            state_shape,
            [IN_VMEM],
            flops=GRAM_FLOPS,
        )(held(sampled, q_way.near if TIE_GRAM else None))
    if NEAR_AT == "gram":
        q_way.exchange_near(state)
    if FORWARD_AT == "gram":
        q_way.forward(state)
    q_way.finish()
    q_second = q_way.put(1)
    q_way.put(2)
    q_all = q_way.put(3)
    state = held(state, {"near": q_way.near, "none": None, "second": q_way.second}[BETWEEN])
    with jax.named_scope("basis"):
        _, basis = call(
            lambda *refs: basis_kernel(BLOCKS, *refs),
            (state_shape, shape((count, size, wide), BF16)),
            [IN_VMEM] * 2,
            flops=BASIS_FLOPS,
            aliases={1: 0},
        )(sampled, state)
    basis = held(basis, q_second if TIE1 == "cores" else None)
    with jax.named_scope("cores"):
        left, value, near_left = call(
            lambda *refs: cores_kernel(n_rows, *refs),
            (
                shape((columns, count * half, deep), BF16),
                shape((columns, size, count * half), F32),
                shape((count, size, deep), BF16),
            ),
            [IN_SMEM] + [IN_VMEM] * 5,
            [vmem((count, wide, deep), BF16)],
            flops=3 * n_rows * count * width * size * columns * width * CORES_SCALE,
            moved=2 * n_rows * (pb.size + count * width * columns * width),
        )(near_t, basis, mid_early, mid_late, panel_whole, target_factors)
    with jax.named_scope("output"):
        near_new, far_new = call(
            lambda *refs: output_kernel(n_rows, *refs),
            (shape(near_blocks.shape, BF16), shape(target_factors.shape, BF16)),
            [IN_SMEM] + [IN_VMEM] * 6,
            flops=2 * columns * size * deep * count * half,
            moved=2 * n_rows * q.size,
        )(near_t, q_all, basis, left, value, near_left, near_blocks)
    return near_new, far_new


def solution(mesh):
    placed = (
        P("rows", "cols", None, None),
        P("cols", None, None),
        P("rows", "cols", None, None),
        P("rows", "cols", None, None),
        P("rows", "cols", None, None),
        P("rows", "cols"),
        P("cols", None, None),
    )
    return jax.shard_map(
        per_device,
        mesh=mesh,
        in_specs=placed,
        out_specs=(P("rows", "cols", None, None), P("rows", "cols", None, None)),
        check_vma=False,
    )
```

```python
import math

import jax
import jax.numpy as jnp
from jax import lax
from jax.experimental import pallas as pl
from jax.experimental.pallas import tpu as pltpu
from jax.sharding import PartitionSpec as P

F32 = jnp.float32
BF16 = jnp.bfloat16
NN = (((1,), (0,)), ((), ()))
NT = (((1,), (1,)), ((), ()))
TN = (((0,), (0,)), ((), ()))
PLACE_VMEM = 1024 * 1024
PLACE_P = 10
PLACE_Q = 1
PLACE_Q0 = 1
PLACE_Q1 = 10
B_AT = "third"
TIE_B = 0
MID_SCALE = 1
SAMPLED_SCALE = 1
BLOCKS = 3
GRAM_FLOPS = int(1e9)
BETWEEN = "second"
CORES_SCALE = 1
TIE0 = 2
TIE_Y = 1
TIE_GRAM = 0
BASIS_FLOPS = int(1e9)
PROJECT_FLOPS = int(1e9)
CORES_FLOPS = int(1e9)
MOST_FLOPS = int(1e9)
TIE_CORES = 1
FORWARD_AT = "gram"
NEAR_AT = "pb"
GATE_ALONG = "third"
GATE_FORWARD = "pb"
TIE1 = "cores"
EARLY_Q = 0
VMEM_BYTES = 14 * 1024 * 1024


def dot(left, right, dims=NN, precision=None):
    return lax.dot_general(left, right, dims, precision=precision, preferred_element_type=F32)


def halves(shape, half):
    return lax.broadcasted_iota(jnp.int32, shape, len(shape) - 1) // half % 2 == 0


def swap(value, half):
    return jnp.concatenate([value[:, half:], value[:, :half]], axis=1)


def call(kernel, out_shape, in_specs, scratch=(), flops=0, moved=0, aliases=None):
    out_specs = jax.tree.map(lambda _: pl.BlockSpec(memory_space=pltpu.VMEM), out_shape)
    return pl.pallas_call(
        kernel,
        out_shape=out_shape,
        in_specs=in_specs,
        out_specs=out_specs,
        scratch_shapes=list(scratch),
        input_output_aliases=aliases or {},
        compiler_params=pltpu.CompilerParams(vmem_limit_bytes=VMEM_BYTES),
        cost_estimate=pl.CostEstimate(flops=flops, bytes_accessed=moved, transcendentals=0),
    )


IN_VMEM = pl.BlockSpec(memory_space=pltpu.VMEM)
IN_SMEM = pl.BlockSpec(memory_space=pltpu.SMEM)
ANYWHERE = pl.BlockSpec(memory_space=pl.ANY)


def pack_rows_kernel(rows_ref, sketch_ref, pb_ref, q_ref):
    _, columns, size, width = rows_ref.shape
    half = width // 2
    for j in range(columns):
        first, second = rows_ref[0, j], rows_ref[1, j]
        lanes = pl.ds(j * width, width)
        pb_ref[:size, lanes] = jnp.concatenate([first[:, :half], second[:, :half]], axis=1)
        q_pair = jnp.concatenate([first[:, half:], second[:, half:]], axis=1)
        q_ref[:, lanes] = q_pair
        pb_ref[pl.ds(size, half), lanes] = dot(sketch_ref[j], q_pair).astype(BF16)


def pack_panel_kernel(panel_ref, inv_ref, out_ref):
    count, pivots, size, width = panel_ref.shape
    half = width // 2
    for k in range(pivots):
        rights = [jnp.transpose(panel_ref[i, k])[half:] for i in range(count)]
        hat = dot(jnp.concatenate(rights, axis=0), inv_ref[k]).astype(BF16)
        for i in range(count):
            start = (k // 2) * count * width + i * width + (k % 2) * half
            out_ref[pl.ds(start, half), :] = hat[i * half : (i + 1) * half]
    base = (pivots // 2) * count * width
    for i in range(count):
        for k in range(0, pivots, 2):
            pair = [panel_ref[i, k + m][:, :half] for m in range(2)]
            out_ref[pl.ds(base + i * size, size), pl.ds(k * half, width)] = jnp.concatenate(pair, axis=1)


def target_sketch(target_ref, sketch_ref, out_ref):
    count, columns, size, width = target_ref.shape
    half = width // 2
    first = halves((half, width), half)
    zero = jnp.zeros((half, width), BF16)
    for i in range(count):
        for j in range(0, columns, 2):
            core = []
            for m in range(2):
                product = dot(sketch_ref[j + m], target_ref[i, j + m])
                core.append(jnp.where(first, swap(product, half), 0.0).astype(BF16))
            left = jnp.concatenate([target_ref[i, j], target_ref[i, j + 1]], axis=1)
            right = jnp.concatenate(
                [jnp.concatenate([core[0], zero], axis=1), jnp.concatenate([zero, core[1]], axis=1)], axis=0
            )
            out_ref[i, :, pl.ds(j * half, width)] = dot(left, right, NT)


def fetch_all(sources, target, owners_ref, sem):
    copies = []
    for n, source in enumerate(sources):
        copies.append(pltpu.make_async_copy(source, target.at[owners_ref[n]], sem.at[n]))
    for copy in copies:
        copy.start()
    return copies


def mid_pair(n_rows, t, blocks, panel_ref, mid_ref, slot, weight_ref):
    _, tall, wide = mid_ref.shape
    count = weight_ref.shape[0]
    width = tall // count
    half = width // 2
    columns = wide // width
    size = blocks[0].shape[0] - half
    row_half = lax.broadcasted_iota(jnp.int32, (tall, 2 * width), 0) // half % 2
    lane_half = lax.broadcasted_iota(jnp.int32, (tall, 2 * width), 1) // half % 2
    same = row_half == lane_half
    zero = jnp.zeros((half, width), BF16)
    first = arrivals(n_rows)(lax.axis_index("rows"), t)
    plane = first // 2
    for m in range(2):
        part = (first + m) % 2
        left = panel_ref[plane, pl.ds(pl.multiple_of(part * tall, tall), tall), :]
        for j in range(0, columns, 2):
            lanes = pl.ds(j * width, 2 * width)
            mid = dot(left, blocks[m][:size, lanes])
            mid = jnp.where(same, mid, 0.0).astype(BF16)
            mid_ref[slot + m, :, lanes] = mid
            b_pair = blocks[m][size:, lanes]
            right = jnp.concatenate(
                [
                    jnp.concatenate([b_pair[:, :width], zero], axis=1),
                    jnp.concatenate([zero, b_pair[:, width:]], axis=1),
                ],
                axis=0,
            )
            product = dot(mid, right, NT).astype(BF16)
            for i in range(count):
                weight_ref[i, pl.ds(pl.multiple_of(part * width, width), width), pl.ds(j * half, width)] = product[
                    i * width : (i + 1) * width
                ]
    return plane


def subtract(total_ref, panel_ref, plane, weight_ref):
    count, size, _ = total_ref.shape
    base = panel_ref.shape[1] - count * size
    for i in range(count):
        total_ref[i] = total_ref[i] - dot(panel_ref[plane, pl.ds(base + i * size, size), :], weight_ref[i])


def mid_kernel(n_rows, n_cols, pb_all, target_ref, sketch_ref, *refs):
    panels = refs[:n_cols]
    mid_ref, total_ref, panel_ref, weight, sem_panel = refs[n_cols:]
    copies = fetch_all(panels, panel_ref, column_owners(n_cols), sem_panel)
    target_sketch(target_ref, sketch_ref, total_ref)
    for copy in copies:
        copy.wait()

    def step(s, carry):
        blocks = pb_all.at[2 * s], pb_all.at[2 * s + 1]
        plane = mid_pair(n_rows, 2 * s, blocks, panel_ref, mid_ref, 2 * s, weight)
        subtract(total_ref, panel_ref, plane, weight)
        return carry

    lax.fori_loop(0, n_rows // 2 - 1, step, 0)


def sampled_kernel(n_rows, first_ref, second_ref, panel_ref, total_ref, mid_ref, sampled_ref, weight):
    plane = mid_pair(n_rows, n_rows - 2, (first_ref, second_ref), panel_ref, mid_ref, 0, weight)
    sampled_ref[...] = total_ref[...]
    subtract(sampled_ref, panel_ref, plane, weight)


def gram_kernel(blocks, sampled_ref, state):
    count, _, wide = sampled_ref.shape
    half, _, width = state.shape
    pairs = wide // width
    first = halves((half, width), half)
    for i in range(count):
        for p in range(pairs):
            z_pair = sampled_ref[i, :, pl.ds(p * width, width)]
            gram = dot(z_pair, z_pair, TN, lax.Precision.HIGHEST)
            state[:, i * pairs + p, :] = jnp.where(first, gram[:half], gram[half:])
    eliminate(state, 0, blocks, math.sqrt(sampled_ref.shape[1]))


def basis_kernel(blocks, sampled_ref, state_in, state, basis_ref):
    count, size, wide = sampled_ref.shape
    half, _, width = state.shape
    pairs = wide // width
    first = halves((half, width), half)
    eliminate(state, blocks, half // 8, math.sqrt(size))
    for i in range(count):
        for p in range(pairs):
            inverse = state[:, i * pairs + p, :]
            inverse = jnp.concatenate([jnp.where(first, inverse, 0.0), jnp.where(first, 0.0, inverse)], axis=0)
            z_pair = sampled_ref[i, :, pl.ds(p * width, width)]
            product = dot(z_pair, inverse, NT, lax.Precision.HIGHEST)
            basis_ref[i, :, pl.ds(p * width, width)] = product.astype(BF16)


def eliminate(state, first_block, last_block, root_size):
    half, held, width = state.shape
    sub = 8
    lane = lax.broadcasted_iota(jnp.int32, (held, width), 1)
    column = lane % half
    origin = lane - column

    def pick(row, pivot):
        return jnp.take_along_axis(row, origin + pivot, axis=1)

    def one_block(block, carry):
        start = block * sub
        rows = [state[start + r] for r in range(sub)]
        core = {(r, s): pick(rows[r], start + s) for r in range(sub) for s in range(r, sub)}
        lines, finals = [], []
        for q in range(sub):
            pivot = start + q
            root = lax.rsqrt(core[q, q])
            inverse = root * root
            finals.append(rows[q])
            unit = jnp.where(column == pivot, 1.0, rows[q])
            state[pivot] = jnp.where(column <= pivot, unit * (root_size * root), 0.0)
            line = unit * inverse
            lines.append(jnp.where(jnp.logical_and(column > pivot, column < start + sub), 0.0, line))
            for r in range(q + 1, sub):
                scaled = core[q, r] * inverse
                rows[r] = jnp.where(column == pivot, 0.0, rows[r]) - core[q, r] * line
                for s in range(r, sub):
                    core[r, s] = core[r, s] - scaled * core[q, s]
        inside = jnp.logical_and(column >= start, column < start + sub)

        def update(v, inner):
            for r in range(sub):
                row = v * sub + r
                value = jnp.where(inside, 0.0, state[row])
                for q in range(sub):
                    value = value - pick(finals[q], row) * lines[q]
                state[row] = value
            return inner

        lax.fori_loop(block + 1, half // sub, update, 0)
        return carry

    lax.fori_loop(first_block, last_block, one_block, 0)


def project_kernel(basis_ref, panel_ref, target_ref, cores_ref, value_ref):
    count, size, _ = basis_ref.shape
    columns, width = target_ref.shape[1], target_ref.shape[3]
    half = width // 2
    n_cols, rows, deep = panel_ref.shape
    base = rows - count * size
    first = halves((half, width), half)
    zero = jnp.zeros((half, width), BF16)
    turned = []
    for i in range(count):
        basis_t = jnp.transpose(basis_ref[i])
        turned.append(basis_t)
        for c in range(n_cols):
            product = dot(basis_t, panel_ref[c, pl.ds(base + i * size, size), :])
            cores_ref[i, :, pl.ds(c * deep, deep)] = product.astype(BF16)
    for i in range(0, count, 2):
        for j in range(columns):
            core = []
            for m in range(2):
                product = dot(turned[i + m][j * half : (j + 1) * half], target_ref[i + m, j])
                core.append(jnp.where(first, 0.0, swap(product, half)).astype(BF16))
            left = jnp.concatenate([target_ref[i, j], target_ref[i + 1, j]], axis=1)
            right = jnp.concatenate(
                [jnp.concatenate([core[0], zero], axis=1), jnp.concatenate([zero, core[1]], axis=1)], axis=0
            )
            value_ref[j, :, pl.ds(i * half, width)] = dot(left, right, NT)


def cores_kernel(n_rows, near_ref, cores_ref, early_ref, late_ref, panel_ref, left_ref, near_left_ref):
    count, wide, _ = cores_ref.shape
    columns = left_ref.shape[0]
    half = wide // columns
    width = 2 * half
    n_cols, rows, deep = panel_ref.shape
    size = near_left_ref.shape[1]
    per_col = deep // width
    base = rows - count * size
    owner = arrivals(n_rows)
    me = lax.axis_index("rows")

    def one_pair(t, mid_ref, slot):
        o = owner(me, t)
        lanes = pl.ds(pl.multiple_of(t * width, width), width)
        from_lanes = pl.ds(pl.multiple_of(o * width, width), width)
        for i in range(count):
            for j in range(columns):
                product = dot(
                    cores_ref[i, pl.ds(j * half, half), from_lanes],
                    mid_ref[slot, pl.ds(i * width, width), pl.ds(j * width, width)],
                )
                left_ref[j, pl.ds(i * half, half), lanes] = product.astype(BF16)
            near = pl.ds(pl.multiple_of(near_ref[0, i] * width, width), width)
            x_part = panel_ref[
                o // per_col, pl.ds(base + i * size, size), pl.ds(pl.multiple_of(o % per_col * width, width), width)
            ]
            near_left_ref[i, :, lanes] = dot(x_part, mid_ref[slot, pl.ds(i * width, width), near]).astype(BF16)

    def step(t, carry):
        one_pair(t, early_ref, t)
        return carry

    lax.fori_loop(0, n_rows - 2, step, 0)
    for m in range(2):
        one_pair(n_rows - 2 + m, late_ref, m)


def last_slot(n_rows):
    if n_rows != 8:
        return n_rows - 2
    me = lax.axis_index("rows")
    return jnp.where((me < 2) | (me > 5), 6, 4)


def most_slots(n_rows):
    return [*range(0, n_rows - 4, 2), 2 * n_rows - 6 - last_slot(n_rows)]


def joined(q_ref, slots, lanes):
    return jnp.concatenate([q_ref[slot + m, :, lanes] for slot in slots for m in range(2)], axis=1)


def lanes_of(slot, width):
    return pl.ds(pl.multiple_of(slot * width, width), 2 * width)


def most_kernel(n_rows, near_ref, q_ref, left_ref, value_ref, near_left_ref, near_block_ref, far_ref, near_sum_ref):
    columns = left_ref.shape[0]
    count = near_left_ref.shape[0]
    width = q_ref.shape[2] // columns
    slots = most_slots(n_rows)
    for j in range(columns):
        right = jnp.concatenate([left_ref[j, :, lanes_of(slot, width)] for slot in slots], axis=1)
        far_ref[j] = value_ref[j] - dot(joined(q_ref, slots, pl.ds(j * width, width)), right, NT)
    for i in range(count):
        near = pl.ds(pl.multiple_of(near_ref[0, i] * width, width), width)
        left = jnp.concatenate([near_left_ref[i, :, lanes_of(slot, width)] for slot in slots], axis=1)
        near_sum_ref[i] = near_block_ref[i, 0].astype(F32) - dot(left, joined(q_ref, slots, near), NT)


def output_kernel(
    n_rows, near_ref, own_ref, other_ref, basis_ref, left_ref, far_ref, near_left_ref, near_sum_ref, near_out_ref, far_out_ref
):
    count, columns, size, width = far_out_ref.shape
    half = width // 2
    root_size = math.sqrt(size)
    first = halves((size, width), half)
    lanes = lanes_of(last_slot(n_rows), width)

    def q_at(columns_at):
        return jnp.concatenate([ref[:, columns_at] for ref in (own_ref, other_ref)], axis=1)

    for j in range(columns):
        q_last = q_at(pl.ds(j * width, width))
        weights = (far_ref[j] - dot(q_last, left_ref[j, :, lanes], NT)) / root_size
        for i in range(count):
            tile = weights[:, i // 2 * width : (i // 2 + 1) * width]
            if i % 2 == 0:
                tile = swap(tile, half)
            basis = basis_ref[i, :, pl.ds(j // 2 * width, width)]
            if j % 2 == 1:
                basis = swap(basis, half)
            block = jnp.where(first, basis, tile.astype(BF16))
            far_out_ref[i, j] = jnp.where(near_ref[0, i] == j, jnp.zeros_like(block), block)
    for i in range(count):
        near = pl.ds(pl.multiple_of(near_ref[0, i] * width, width), width)
        update = dot(near_left_ref[i, :, lanes], q_at(near), NT)
        near_out_ref[i, 0] = (near_sum_ref[i] - update).astype(BF16)


def arrivals(n):
    if n != 8:
        return lambda me, t: t
    third = lambda me: jnp.where(me < 4, 4, 2) + me % 2
    fourth = lambda me: jnp.where(me < 4, 6, 0) + me % 2

    def owner(me, t):
        base = jnp.where(t < 2, me, jnp.where(t < 4, me ^ 2, jnp.where(t < 6, third(me), fourth(me))))
        return base ^ (t % 2)

    return owner


def held(value, *events):
    events = [event for event in events if event is not None]
    return lax.optimization_barrier((value,) + tuple(events))[0] if events else value


def place(buffer, t, blocks, n, micros):
    def kernel(*refs):
        sources, target, sem = refs[:2], refs[-2], refs[-1]
        slot = t(lax.axis_index("rows")) if callable(t) else t
        copies = fetch_all(sources, target, [slot, slot + 1], sem)
        for copy in copies:
            copy.wait()

    given = [] if buffer is None else [buffer]
    return pl.pallas_call(
        kernel,
        out_shape=jax.ShapeDtypeStruct((n,) + blocks[0].shape, blocks[0].dtype),
        in_specs=[IN_VMEM] * (2 + len(given)),
        out_specs=IN_VMEM,
        scratch_shapes=[pltpu.SemaphoreType.DMA((2,))],
        input_output_aliases={2: 0} if given else {},
        compiler_params=pltpu.CompilerParams(vmem_limit_bytes=1024 * 1024),
        cost_estimate=pl.CostEstimate(flops=int(micros * 1.15e9), bytes_accessed=0, transcendentals=0),
    )(*blocks, *given)


class Gather:
    slots = [0, 2, 4, 6]
    inner = [(2, 4), (4, 2), (3, 5), (5, 3)]
    outward = [(2, 0), (3, 1), (4, 6), (5, 7)]

    def __init__(self, block, micros):
        self.n = lax.axis_size("rows")
        self.block, self.micros, self.whole = block, micros, None
        me = lax.axis_index("rows")
        self.is_end = jnp.logical_or(me < 2, me >= self.n - 2)

    def send(self, value, pairs):
        return lax.ppermute(value, "rows", pairs)

    def flip(self, value, bits):
        return self.send(value, [(i, i ^ bits) for i in range(self.n)])

    def start_across(self, *events):
        self.x_own = self.flip(held(self.block, *events), 1)

    def start_along(self, *events):
        block = held(self.block, *events)
        self.near, self.mid = self.flip(block, 2), self.send(block, self.inner)

    def forward(self, *events):
        self.x_near = self.flip(held(self.near, *events), 1)
        self.far = self.send(held(self.near, *events), self.inner)
        out = self.send(held(self.mid, *events), self.outward)
        self.second = jnp.where(self.is_end, out, self.mid)

    def forward_again(self, *events):
        self.x_second = self.flip(held(self.second, *events), 1)
        out = self.send(held(self.far, *events), self.outward)
        self.third = jnp.where(self.is_end, out, self.far)

    def finish(self, *events):
        self.x_third = self.flip(held(self.third, *events), 1)

    def put(self, stage, *events):
        pair = [
            lambda: (self.block, self.x_own),
            lambda: (self.near, self.x_near),
            lambda: (self.second, self.x_second),
            lambda: (self.third, self.x_third),
        ][stage]()
        pair = (pair[0], held(pair[1], *events)) if stage == 0 else pair
        whole = self.whole if stage == 0 or all(event is None for event in events) else held(self.whole, *events)
        self.whole = place(whole, self.slots[stage], pair, self.n, self.micros)
        return self.whole

    def last(self):
        return self.third, self.x_third

    def last_but_one(self):
        return self.x_second


class DirectGather(Gather):
    slots = [0, 2, lambda me: jnp.where((me < 2) | (me > 5), 4, 6), lambda me: jnp.where((me < 2) | (me > 5), 6, 4)]

    def start_along(self, *events):
        block = held(self.block, *events)
        self.second, self.near = self.flip(block, 4), self.flip(block, 2)

    def exchange_near(self, *events):
        self.x_near = self.flip(held(self.near, *events), 1)

    def forward(self, *events):
        out = self.send(held(self.second, *events), self.outward)
        self.x_second = self.flip(held(self.second, *events), 1)
        self.third = jnp.where(self.is_end, out, self.middle)

    def cross_middle(self, *events):
        self.middle = self.send(held(self.block, *events), self.inner)


class PlainGather:
    def __init__(self, block, micros):
        self.block = self.near = self.second = self.third = self.far = block
        self.whole = None

    def start_across(self, *events):
        pass

    start_along = forward = forward_again = finish = exchange_near = cross_middle = start_across

    def last_but_one(self):
        return self.block

    def last(self):
        return self.put(0)[-2], self.whole[-1]

    def put(self, stage, *events):
        if self.whole is None:
            self.whole = lax.all_gather(self.block, "rows")
        return self.whole


def column_owners(n):
    me = lax.axis_index("cols")
    return [me ^ t for t in range(n)] if n == 4 else list(range(n))


def gather_cols(block):
    n = lax.axis_size("cols")
    if n != 4:
        whole = lax.all_gather(block, "cols")
        return [whole[o] for o in range(n)]
    core = [(i, i ^ 1) for i in range(n)]
    other = [(i, i ^ 2) for i in range(n)]
    y = lax.ppermute(block, "cols", other)
    own = lax.ppermute(block, "cols", core)
    return [block, own, y, lax.ppermute(y, "cols", core)]


def per_device(panel_cols, pivot_inv, pivot_rows, target_factors, near_blocks, near_cols, sketch):
    n_rows, n_cols = lax.axis_size("rows"), lax.axis_size("cols")
    count, pivots, size, width = panel_cols.shape
    owned, columns = pivot_rows.shape[:2]
    half = width // 2
    wide = columns * half
    assert owned == 2 and columns % 2 == 0 and count % 2 == 0 and pivots % 2 == 0
    assert near_cols.shape[1] == 1
    shape = jax.ShapeDtypeStruct
    sketch_t = jnp.swapaxes(sketch, 1, 2)
    near_t = near_cols.T

    with jax.named_scope("pack_rows"):
        pb, q = call(
            pack_rows_kernel,
            (shape((size + half, columns * width), BF16), shape((size, columns * width), BF16)),
            [IN_VMEM] * 2,
            flops=2 * columns * half * size * width,
            moved=4 * pivot_rows.size,
        )(pivot_rows, sketch_t)
    panel_rows = (pivots // 2) * count * width + count * size
    with jax.named_scope("pack_panel"):
        panel = call(
            pack_panel_kernel,
            shape((panel_rows, pivots * half), BF16),
            [IN_VMEM] * 2,
            flops=2 * count * pivots * half * size * size,
            moved=4 * panel_cols.size,
        )(panel_cols, pivot_inv)
    panels = gather_cols(panel)
    vmem = pltpu.VMEM
    deep = n_rows * width
    mid_flops = 4 * count * width * size * columns * width
    weight_scratch = vmem((count, 2 * width, wide), BF16)

    def mids(arrived, target):
        with jax.named_scope("mid"):
            return call(
                lambda *refs: mid_kernel(n_rows, n_cols, *refs),
                (
                    shape((n_rows - 2, count * width, columns * width), BF16),
                    shape((count, size, wide), F32),
                    shape((n_cols,) + panel.shape, BF16),
                ),
                [IN_VMEM] * 3 + [ANYWHERE] * n_cols,
                [weight_scratch, pltpu.SemaphoreType.DMA((n_cols,))],
                flops=mid_flops * (n_rows - 2) * MID_SCALE,
            )(arrived, target, sketch_t, *panels)

    kind = Gather if n_rows == 8 else PlainGather
    pb_way = kind(pb, PLACE_P)
    q_way = (DirectGather if n_rows == 8 else kind)(q, PLACE_Q)
    pb_way.start_along()
    pb_way.start_across()
    pb_way.forward()
    if TIE0 < 3:
        q_way.start_across(pb_way.near)
    pb_way.forward_again()
    pb_way.finish()
    pb_way.put(0, panels[2] if TIE_Y == 2 else None)
    q_way.micros = PLACE_Q0
    q_first = q_way.put(0) if TIE0 < 3 else None
    pb_way.put(1, q_first if TIE0 == 1 else None, panels[2] if TIE_Y == 1 else None)
    arrived = pb_way.put(2, q_first if TIE0 == 2 else None)
    q_way.micros = PLACE_Q
    if B_AT == "near":
        q_way.cross_middle(pb_way.near, pb_way.mid)
    if B_AT == "far":
        q_way.cross_middle(pb_way.far)
    if B_AT == "second":
        q_way.cross_middle(pb_way.second)
    if B_AT == "third":
        q_way.cross_middle(pb_way.third)
    if B_AT == "pb":
        q_way.cross_middle(pb_way.x_third if n_rows == 8 else None)
    if n_rows == 8 and TIE_B:
        arrived = held(arrived, q_way.middle)
    mid_early, total, panel_whole = mids(arrived, held(target_factors, pb_way.far))
    if GATE_ALONG == "both":
        q_way.start_along(pb_way.third, pb_way.last_but_one())
    if GATE_ALONG == "third":
        q_way.start_along(pb_way.third)
    if GATE_ALONG == "mid":
        q_way.start_along(total)
    if GATE_ALONG == "far":
        q_way.start_along(pb_way.far)
    pb_done = pb_way.last()[1]
    if TIE0 == 3:
        q_way.start_across(pb_done)
        q_way.put(0)
    with jax.named_scope("sampled"):
        mid_late, sampled = call(
            lambda *refs: sampled_kernel(n_rows, *refs),
            (shape((2,) + mid_early.shape[1:], BF16), shape((count, size, wide), F32)),
            [IN_VMEM] * 4,
            [weight_scratch],
            flops=mid_flops * 2 * SAMPLED_SCALE,
        )(*pb_way.last(), panel_whole, total)
    if NEAR_AT != "gram":
        q_way.exchange_near({"pb": pb_done, "sampled": sampled}[NEAR_AT])
    if FORWARD_AT == "pb":
        q_way.forward(pb_done)
    state_shape = shape((half, -(-count * columns // 2 // 8) * 8, width), F32)
    with jax.named_scope("gram"):
        state = call(
            lambda *refs: gram_kernel(BLOCKS, *refs),
            state_shape,
            [IN_VMEM],
            flops=GRAM_FLOPS,
        )(held(sampled, q_way.near if TIE_GRAM else None))
    if NEAR_AT == "gram":
        q_way.exchange_near(state)
    if FORWARD_AT == "gram":
        q_way.forward(state)
    q_way.micros = PLACE_Q1
    q_near = q_way.put(1)
    q_way.micros = PLACE_Q
    state = held(state, *{"near": [q_way.near], "none": [], "second": [q_way.second], "put": [q_near, q_way.second]}[BETWEEN])
    with jax.named_scope("basis"):
        _, basis = call(
            lambda *refs: basis_kernel(BLOCKS, *refs),
            (state_shape, shape((count, size, wide), BF16)),
            [IN_VMEM] * 2,
            flops=BASIS_FLOPS,
            aliases={1: 0},
        )(sampled, state)
    q_most = q_way.put(2)
    with jax.named_scope("project"):
        cores, value = call(
            project_kernel,
            (shape((count, wide, deep), BF16), shape((columns, size, count * half), F32)),
            [IN_VMEM] * 3,
            flops=PROJECT_FLOPS,
        )(held(basis, q_near if TIE1 == "near" else None), panel_whole, target_factors)
    with jax.named_scope("cores"):
        left, near_left = call(
            lambda *refs: cores_kernel(n_rows, *refs),
            (shape((columns, count * half, deep), BF16), shape((count, size, deep), BF16)),
            [IN_SMEM] + [IN_VMEM] * 4,
            flops=CORES_FLOPS,
        )(near_t, held(cores, q_way.third if TIE_CORES else None), mid_early, mid_late, panel_whole)
    with jax.named_scope("most"):
        far_sum, near_sum = call(
            lambda *refs: most_kernel(n_rows, *refs),
            (shape((columns, size, count * half), F32), shape((count, size, size), F32)),
            [IN_SMEM] + [IN_VMEM] * 5,
            flops=MOST_FLOPS,
        )(near_t, q_most, left, value, near_left, near_blocks)
    q_way.finish()
    with jax.named_scope("output"):
        near_new, far_new = call(
            lambda *refs: output_kernel(n_rows, *refs),
            (shape(near_blocks.shape, BF16), shape(target_factors.shape, BF16)),
            [IN_SMEM] + [IN_VMEM] * 7,
            flops=2 * columns * size * deep * count * half,
        )(near_t, *q_way.last(), basis, left, far_sum, near_left, near_sum)
    return near_new, far_new


def solution(mesh):
    placed = (
        P("rows", "cols", None, None),
        P("cols", None, None),
        P("rows", "cols", None, None),
        P("rows", "cols", None, None),
        P("rows", "cols", None, None),
        P("rows", "cols"),
        P("cols", None, None),
    )
    return jax.shard_map(
        per_device,
        mesh=mesh,
        in_specs=placed,
        out_specs=(P("rows", "cols", None, None), P("rows", "cols", None, None)),
        check_vma=False,
    )
```
